32 devices in a mesh: dp: 16 (over z, y, core), tensor: 2 (over x).
Axes of the slice: x: 2, y: 2, z: 4, core: 2. Of those that a mesh axis runs over, the one named last changes fastest.
Arguments:
- tokens: bfloat16 [6144, 4096], P('dp'), may hold values from -6 to 6
- doc_lengths: int32 [32], P('dp'), may hold values from 1 to 192, as said below
- gate_weight: bfloat16 [4096, 7168], P('dp', 'tensor'), may hold values from -0.09375 to 0.09375
- up_weight: bfloat16 [4096, 7168], P('dp', 'tensor'), may hold values from -0.09375 to 0.09375
- hidden_grad: bfloat16 [6144, 7168], P('dp', 'tensor'), may hold values from -6 to 6
- in_projector: bfloat16 [64, 4096], replicated, may hold values from -0.09375 to 0.09375
- gate_projector: bfloat16 [64, 7168], P(None, 'tensor'), may hold values from -0.0625 to 0.0625
- up_projector: bfloat16 [64, 7168], P(None, 'tensor'), may hold values from -0.0625 to 0.0625
Outputs:
- gate_features: float32 [32, 64, 64], P('dp', None, 'tensor')
- up_features: float32 [32, 64, 64], P('dp', None, 'tensor')
The draws below stay inside these ranges and needn't reach their ends.
Inputs may be any that keep to these rules, and one draw needn't show every extreme that they name: `doc_lengths`: at least one document in every draw has all 192 slots used.
All inputs are finite; a program needn't handle non-finite values.
Results may differ from the reference program's by a relative error of at most 0.013.
Values may be sent and summed in bfloat16 or wider, within the bound.
No kernel may reach another device: no remote copies, remote signals or barrier semaphores. Data moves between devices by JAX's collectives and lax.ppermute only.
A program may use at most 128 MiB of HBM per device.

```python
import jax
import jax.numpy as jnp
from jax import lax

D = 4096
FF = 7168
R = 64
DOC_LEN = 192
DOCS = 32
TOKENS = 6144


def draw_doc_lengths(key, part):
    key = jax.random.fold_in(key, 5)
    first, second = jax.random.split(key)
    lengths = jax.random.randint(first, (DOCS,), 1, DOC_LEN + 1)
    where = jax.random.randint(second, (), 0, DOCS)
    return jnp.where(jnp.arange(DOCS) == where, DOC_LEN, lengths).astype(jnp.int32)


def level_of(key, dims, cuts, low, largest):
    gain, own = 1.0, jax.random.fold_in(key, 6)
    for dim, blocks in cuts:
        steps = jnp.exp(jax.random.uniform(jax.random.fold_in(own, dim), (blocks,), jnp.float32, low / len(cuts), largest / len(cuts)))
        gain = gain * jnp.repeat(steps, dims[dim] // blocks).reshape([-1 if axis == dim else 1 for axis in range(len(dims))])
    return gain


def normal_values(own_key, extent, deviation, bound, shards=(), held_as=jnp.bfloat16):
    drawn = jax.random.normal(own_key, extent, jnp.float32) * deviation
    if len(shards) > 0:
        drawn = level_of(own_key, extent, shards, -0.22, 0.18) * drawn
    return jnp.clip(drawn, min=-bound, max=bound).astype(held_as)


def setup_inputs(seed: int = 0) -> dict:
    key_list = jax.random.split(jax.random.key(seed), 9)
    tokens = normal_values(key_list[0], (TOKENS, D), 1.0, 6.0, ((0, 16),))
    doc_lengths = draw_doc_lengths(jax.random.fold_in(key_list[8], 71), 0)
    gate_weight = normal_values(key_list[2], (D, FF), D ** -0.5, 0.09375, ((0, 16), (1, 2)))
    up_weight = normal_values(key_list[3], (D, FF), D ** -0.5, 0.09375, ((0, 16), (1, 2)))
    hidden_grad = normal_values(key_list[4], (TOKENS, FF), 1.0, 6.0, ((0, 16), (1, 2)))
    in_projector = normal_values(key_list[5], (R, D), D ** -0.5, 0.09375)
    gate_projector = normal_values(key_list[6], (R, FF), FF ** -0.5, 0.0625, ((1, 2),))
    up_projector = normal_values(key_list[7], (R, FF), FF ** -0.5, 0.0625, ((1, 2),))
    return {"tokens": tokens, "doc_lengths": doc_lengths, "gate_weight": gate_weight, "up_weight": up_weight, "hidden_grad": hidden_grad, "in_projector": in_projector, "gate_projector": gate_projector, "up_projector": up_projector}


def contract_last(left, right):
    return lax.dot_general(left, right, (((1,), (1,)), ((), ())), preferred_element_type=jnp.float32)


def per_document(inputs, side):
    left = inputs.astype(jnp.float32).reshape(DOCS, DOC_LEN, R)
    right = side.astype(jnp.float32).reshape(DOCS, DOC_LEN, R)
    return 0.0625 * jnp.einsum("ntr,nts->nrs", left, right, precision=lax.Precision.HIGHEST)


def reference(tokens, doc_lengths, gate_weight, up_weight, hidden_grad, in_projector, gate_projector, up_projector):
    gate = jnp.dot(tokens, gate_weight, preferred_element_type=jnp.float32)
    up = jnp.dot(tokens, up_weight, preferred_element_type=jnp.float32)
    sig = jax.nn.sigmoid(gate)
    cotangent = hidden_grad.astype(jnp.float32)
    grad_gate = (cotangent * up * sig * (1.0 + gate * (1.0 - sig))).astype(jnp.bfloat16)
    grad_up = (cotangent * gate * sig).astype(jnp.bfloat16)
    position = jnp.arange(TOKENS, dtype=jnp.int32)
    owner = position // DOC_LEN
    within = position % DOC_LEN
    mask = (within < doc_lengths[owner]).astype(jnp.bfloat16)
    inputs = contract_last(tokens, in_projector).astype(jnp.bfloat16) * mask[:, None]
    gate_side = contract_last(grad_gate, gate_projector).astype(jnp.bfloat16)
    up_side = contract_last(grad_up, up_projector).astype(jnp.bfloat16)
    return per_document(inputs, gate_side), per_document(inputs, up_side)
```

```python
import functools

import jax
import jax.numpy as jnp
from jax import lax
from jax.experimental import pallas as pl
from jax.experimental.pallas import tpu as pltpu
from jax.sharding import PartitionSpec as P

DOC_LEN = 192
VMEM_LIMIT = 46 * 1024 * 1024
UNITS = 7
UNITS_A = 3


def contract_last(left, right):
    return lax.dot_general(
        left, right, (((1,), (1,)), ((), ())), preferred_element_type=jnp.float32
    )


def per_document(inputs, side):
    docs = inputs.shape[0] // DOC_LEN
    left = inputs.reshape(docs, DOC_LEN, inputs.shape[1])
    right = side.reshape(docs, DOC_LEN, side.shape[1])
    return 0.0625 * jnp.einsum("ntr,nts->nrs", left, right, preferred_element_type=jnp.float32)


def shards_any(
    tokens,
    doc_lengths,
    gate_weight,
    up_weight,
    hidden_grad,
    in_projector,
    gate_projector,
    up_projector,
):
    def add_one(piece):
        return jnp.dot(tokens, piece, preferred_element_type=jnp.float32)

    gate = add_one(lax.all_gather(gate_weight, "dp", axis=0, tiled=True))
    up = add_one(lax.all_gather(up_weight, "dp", axis=0, tiled=True))
    sig = jax.nn.sigmoid(gate)
    cotangent = hidden_grad.astype(jnp.float32)
    grad_gate = (cotangent * up * sig * (1.0 + gate * (1.0 - sig))).astype(jnp.bfloat16)
    grad_up = (cotangent * gate * sig).astype(jnp.bfloat16)
    rows = tokens.shape[0]
    within = jnp.arange(rows, dtype=jnp.int32) % DOC_LEN
    limits = jnp.repeat(doc_lengths, DOC_LEN)
    mask = (within < limits).astype(jnp.bfloat16)
    projected = contract_last(tokens, in_projector)
    inputs = projected.astype(jnp.bfloat16) * mask[:, None]
    gate_part = contract_last(grad_gate, gate_projector)
    up_part = contract_last(grad_up, up_projector)
    gate_full, up_full = lax.psum((gate_part, up_part), "tensor")
    share = gate_full.shape[1] // lax.axis_size("tensor")
    start = lax.axis_index("tensor") * share
    gate_sum = lax.dynamic_slice_in_dim(gate_full, start, share, 1)
    up_sum = lax.dynamic_slice_in_dim(up_full, start, share, 1)
    gate_side = gate_sum.astype(jnp.bfloat16)
    up_side = up_sum.astype(jnp.bfloat16)
    return (per_document(inputs, gate_side), per_document(inputs, up_side))


def vmem_spec():
    return pl.BlockSpec(memory_space=pltpu.VMEM)


def hbm_spec():
    return pl.BlockSpec(memory_space=pltpu.HBM)


def smem_spec():
    return pl.BlockSpec(memory_space=pltpu.SMEM)


def ffn_kernel(cfg, idx, *refs):
    refs = list(refs)
    groups, final = cfg["groups"], cfg["final"]
    block_refs = [refs.pop(0) for _ in range(cfg["n_blocks"])]
    token_refs = [refs.pop(0) for _ in range(cfg["n_tokens"])]
    held = [refs.pop(0) for _ in cfg["held"]]
    if final:
        grad_refs = [refs.pop(0) for _ in cfg["grads"]]
        gate_proj, up_proj = refs.pop(0), refs.pop(0)
    prev = [refs.pop(0) for _ in range(cfg["prev"])]
    outs = [refs.pop(0) for _ in range(cfg["n_outs"])]
    block_buffer, block_sem = refs.pop(0), refs.pop(0)
    token_buffer, token_sem = refs.pop(0), refs.pop(0)
    if held:
        held_buffer, held_sem = refs.pop(0), refs.pop(0)
    if final:
        grad_buffer, grad_sem = refs
    else:
        out_buffer, out_sem = refs
    core = idx[0]
    deep, width, rows = cfg["deep"], cfg["width"], cfg["rows"]

    def token_copy(slot, unit, at):
        g, d = unit
        ref, z = token_refs[cfg["tokens"][g][d]], idx[1 + cfg["planes"][at]]
        if len(ref.shape) == 2:
            source = ref.at[:, pl.ds(pl.multiple_of(z * deep, deep), deep)]
        else:
            start = pl.multiple_of((z % 2) * deep, deep)
            source = ref.at[2 * (core ^ (d & 1)) + z // 2, :, pl.ds(start, deep)]
        return pltpu.make_async_copy(source, token_buffer.at[slot], token_sem.at[slot])

    def arrived(buffer, sem, slot):
        pltpu.make_async_copy(buffer.at[slot], buffer.at[slot], sem.at[slot]).wait()

    def out_copy(n):
        return pltpu.make_async_copy(out_buffer.at[n % 2], outs[0].at[n], out_sem.at[n % 2])

    kept = [ref.at[i] for ref, count in zip(held, cfg["held"]) for i in range(count)]
    kept = [kept[i] for i in cfg["order"]]

    def grad_copy(n, unit):
        ref, (row, column) = grad_refs[4 * unit[0] + unit[1]], cfg["grads"][4 * unit[0] + unit[1]]
        source = ref.at[pl.ds(row, rows), pl.ds(column, width)]
        return pltpu.make_async_copy(source, grad_buffer.at[n], grad_sem.at[n])

    def finish(group, r, n, both):
        s, d = group["units"][0]
        d = d + r
        arrived(grad_buffer, grad_sem, n)
        gate, up = both[:, :width], both[:, width:]
        sig = 1.0 / (1.0 + jnp.exp(-gate))
        cotangent = grad_buffer[n].astype(jnp.float32)
        grad_gate = (cotangent * up * sig * (1.0 + gate * (1.0 - sig))).astype(jnp.bfloat16)
        grad_up = (cotangent * gate * sig).astype(jnp.bfloat16)
        part = contract_last(gate_proj[...], grad_gate)
        part += contract_last(up_proj[...], grad_up)
        outs[s][d] = prev[s][d] + part if s < len(prev) else part

    def work():
        slot, n_kept, n, asked = 0, 0, 0, set()
        for group in groups:
            for unit in group["units"]:
                for at in group["blocks"]:
                    if at not in asked:
                        asked.add(at)
                        pltpu.make_async_copy(
                            block_refs[at], block_buffer.at[at], block_sem.at[at]
                        ).start()
                    token_copy(slot, unit, at).start()
                    slot += 1
                if group["held"]:
                    pltpu.make_async_copy(
                        kept[n_kept], held_buffer.at[n_kept], held_sem.at[n_kept]
                    ).start()
                    n_kept += 1
                if final:
                    grad_copy(n, unit).start()
                n += 1
        slot, n_kept, first, here = 0, 0, 0, set()
        for group in groups:
            size, count = len(group["blocks"]), len(group["units"])
            fresh = [at for at in group["blocks"] if at not in here]
            here.update(fresh)

            def unit_step(
                r, carry, group=group, size=size, fresh=fresh, slot=slot, n_kept=n_kept, first=first
            ):
                both = None
                for i, at in enumerate(group["blocks"]):
                    if at in fresh:

                        @pl.when(r == 0)
                        def _(at=at):
                            arrived(block_buffer, block_sem, at)

                    arrived(token_buffer, token_sem, slot + r * size + i)
                    term = jnp.dot(
                        token_buffer[slot + r * size + i],
                        block_buffer[at],
                        preferred_element_type=jnp.float32,
                    )
                    both = term if both is None else both + term
                if group["held"]:
                    arrived(held_buffer, held_sem, n_kept + r)
                    both = both + held_buffer[n_kept + r].astype(jnp.float32)
                n = first + r
                if final:
                    finish(group, r, n, both)
                else:

                    @pl.when(n >= 2)
                    def _():
                        out_copy(n - 2).wait()

                    out_buffer[n % 2] = both.astype(out_buffer.dtype)
                    out_copy(n).start()
                return carry

            lax.fori_loop(0, count, unit_step, 0)
            slot, first = slot + size * count, first + count
            if group["held"]:
                n_kept += count
        if not final:
            out_copy(first - 2).wait()
            out_copy(first - 1).wait()

    runs = idx[5] == cfg["inner"]
    pl.when(runs)(work)

    if final:

        @pl.when(jnp.logical_not(runs))
        def _():
            for s, out in enumerate(outs):
                out[...] = prev[s][...] if s < len(prev) else jnp.zeros_like(out)


TOKENS = ((0, 1, 2, 2), (3, 3, 4, 4))


def group(units, blocks, held=False):
    return {"units": units, "blocks": blocks, "held": held}


def ffn(idx, inner, blocks, tokens, groups, held, grads, proj, prev, name, order=None):
    deep, width = blocks[0][0].shape[0], blocks[0][0].shape[1] // 2
    rows = tokens[0].shape[-2]
    final = grads is not None
    n_units = sum(len(one["units"]) for one in groups)
    cfg = {
        "inner": inner,
        "planes": [plane for _, plane in blocks],
        "tokens": TOKENS,
        "n_blocks": len(blocks),
        "n_tokens": len(tokens),
        "groups": groups,
        "held": [value.shape[0] for value in held],
        "order": order or range(sum(value.shape[0] for value in held)),
        "grads": [place for _, *place in grads or ()],
        "final": final,
        "n_outs": len(grads) // 4 if final else 1,
        "prev": len(prev),
        "deep": deep,
        "width": width,
        "rows": rows,
    }
    large = [*(block for block, _ in blocks), *tokens, *held, *(one[0] for one in grads or ())]
    args = [pltpu.with_memory_space_constraint(value, pltpu.HBM) for value in large]
    specs = [hbm_spec()] * len(args)
    args += [*(proj if final else ()), *prev]
    specs += [vmem_spec()] * (len(args) - len(specs))
    if final:
        shapes = [(4, proj[0].shape[0], rows)] * (len(grads) // 4)
    else:
        shapes = [(n_units, rows, 2 * width)]
    if final:
        results = [jax.ShapeDtypeStruct(shape, jnp.float32) for shape in shapes]
    else:
        results = [pltpu.HBM(shape, jnp.bfloat16) for shape in shapes]

    def buffers(count, shape, dtype, first=rows):
        return [pltpu.VMEM((count, first, shape), dtype), pltpu.SemaphoreType.DMA((count,))]

    slots = sum(len(one["units"]) * len(one["blocks"]) for one in groups)
    scratch = buffers(len(blocks), 2 * width, jnp.bfloat16, deep)
    scratch += buffers(slots, deep, jnp.bfloat16)
    if held:
        scratch += buffers(sum(cfg["held"]), 2 * width, jnp.bfloat16)
    if final:
        scratch += buffers(n_units, width, jnp.bfloat16)
    else:
        scratch += buffers(2, 2 * width, jnp.bfloat16)
    parts = pl.pallas_call(
        functools.partial(ffn_kernel, cfg),
        out_shape=results,
        in_specs=[smem_spec()] + specs,
        out_specs=[vmem_spec() if final else hbm_spec()] * len(shapes),
        scratch_shapes=scratch,
        compiler_params=pltpu.CompilerParams(vmem_limit_bytes=VMEM_LIMIT),
        cost_estimate=pl.CostEstimate(flops=1, bytes_accessed=1, transcendentals=0),
        name=name,
    )(idx, *args)
    return list(parts)


def features_kernel(docs, mine, sent, projected, limits, gate_out, up_out):
    side = (mine[...] + sent[...].astype(jnp.float32)).astype(jnp.bfloat16)
    share = side.shape[0] // 2
    inputs = projected[...].astype(jnp.bfloat16)
    position = lax.broadcasted_iota(jnp.int32, inputs.shape, 1)
    for n in range(docs):
        within = position - n * DOC_LEN
        used = jnp.logical_and(within >= 0, within < limits[n])
        left = jnp.where(used, inputs, jnp.zeros_like(inputs))
        gate_out[n] = 0.0625 * contract_last(side[:share], left)
        up_out[n] = 0.0625 * contract_last(side[share:], left)


def shards_planes(
    tokens,
    doc_lengths,
    gate_weight,
    up_weight,
    hidden_grad,
    in_projector,
    gate_projector,
    up_projector,
):
    dp, x = lax.axis_index("dp"), lax.axis_index("tensor")
    z, q = dp // 4, dp % 4
    inner = jnp.logical_or(z == 1, z == 2).astype(jnp.int32)
    first_pair = z < 2
    far_inner = jnp.where(first_pair, 2, 1)
    far_outer = jnp.where(first_pair, 3, 0)
    y, core = (dp // 2) % 2, dp % 2
    idx = jnp.stack([core, z, z ^ 1, far_inner, far_outer, inner]).astype(jnp.int32)

    def planes(pairs):
        return [(4 * a + i, 4 * b + i) for a, b in pairs for i in range(4)]

    inward, outward = planes([(0, 1), (3, 2)]), planes([(1, 0), (2, 3)])
    middle, neighbours = planes([(1, 2), (2, 1)]), planes([(0, 1), (1, 0), (2, 3), (3, 2)])

    def move(value, perm):
        return lax.ppermute(value, "dp", perm)

    def flip(value, d):
        return lax.ppermute(value, "dp", [(i, i ^ d) for i in range(16)])

    def across(value):
        return lax.ppermute(value, "tensor", [(0, 1), (1, 0)])

    def gather_chips(value):
        groups = [[4 * pair + i for i in range(4)] for pair in range(8)]
        return lax.all_gather(value, ("dp", "tensor"), axis_index_groups=groups)

    rows, model = tokens.shape
    depth, hidden = gate_weight.shape
    quarter = hidden // 4
    cut = quarter // UNITS * UNITS_A
    chunk_a, chunk_b = slice(0, cut), slice(cut, quarter)
    ranks = gate_projector.shape[0]
    share = ranks // 2

    clock = idx

    def wait(*values):
        nonlocal clock
        *values, clock = lax.optimization_barrier((*values, clock))
        return values[0] if len(values) == 1 else values

    def quarter_of(value, d):
        return lax.dynamic_slice_in_dim(value, (q ^ d) * quarter, quarter, 1)

    def weights_for(d, chunk):
        gate, up = quarter_of(gate_weight, d), quarter_of(up_weight, d)
        return jnp.concatenate([gate[:, chunk], up[:, chunk]], axis=1)

    def grads_for(d, chunk):
        return quarter_of(hidden_grad, d)[:, chunk]

    def by_core(mine, other):
        first, second = jnp.where(core == 0, mine, other), jnp.where(core == 0, other, mine)
        return jnp.concatenate([first, second], axis=0)

    def by_y(mine, other, columns):
        mine, other = mine[:, columns], other[:, columns]
        first, second = jnp.where(y == 0, mine, other), jnp.where(y == 0, other, mine)
        return jnp.concatenate([first, second], axis=0)

    gate_mine = lax.dynamic_slice_in_dim(gate_projector, q * quarter, quarter, 1)
    up_mine = lax.dynamic_slice_in_dim(up_projector, q * quarter, quarter, 1)
    nothing = jnp.zeros((share, quarter), jnp.bfloat16)
    gate_rows = jnp.concatenate([gate_mine[:share], nothing, gate_mine[share:], nothing], axis=0)
    up_rows = jnp.concatenate([nothing, up_mine[:share], nothing, up_mine[share:]], axis=0)
    proj_a = [gate_rows[:, chunk_a], up_rows[:, chunk_a]]
    proj_b = [gate_rows[:, chunk_b], up_rows[:, chunk_b]]

    wide_a, wide_b = slice(0, 2 * cut), slice(2 * cut, 2 * quarter)
    both = [
        jnp.concatenate([weights_for(d, chunk_a), weights_for(d, chunk_b)], axis=1) for d in range(4)
    ]
    half = lax.dynamic_slice_in_dim(tokens, x * (model // 2), model // 2, 1)
    core_in = flip(both[1], 1)
    both[2], both[3], half, core_in = wait(both[2], both[3], half, core_in)
    side_in, cross_in = flip(both[2], 2), flip(both[3], 3)
    end_half = move(half, inward)
    u0 = by_core(both[0], core_in)
    far_u0 = move(u0, middle)
    core_tokens = flip(tokens, 1)
    grads = [quarter_of(hidden_grad, d) for d in range(4)]
    grads_out_a = [piece[:, chunk_a] for piece in grads[2:]]
    grads_out_b = jnp.stack([piece[:, chunk_b] for piece in grads[2:]])
    core_grads = flip(grads[1], 1)
    projected = contract_last(in_projector, tokens)

    side_in, cross_in, far_u0, end_half, half, core_tokens, projected = wait(
        side_in, cross_in, far_u0, end_half, half, core_tokens, projected
    )
    grads_out_a[0], grads_out_a[1], grads_out_b, core_grads, grads[0] = wait(
        *grads_out_a, grads_out_b, core_grads, grads[0]
    )
    proj_a[0], proj_a[1], proj_b[0], proj_b[1] = wait(*proj_a, *proj_b)
    u1 = by_core(side_in, cross_in)
    far_u1 = move(u1, middle)
    whole_a = by_y(u0, u1, wide_a)
    end_a = move(whole_a, neighbours)
    side_half = flip(half, 2)
    end_all = gather_chips(end_half)
    whole_b = by_y(u0, u1, wide_b)

    far_u1, end_a, side_half, whole_b, end_half, grads_out_b = wait(
        far_u1, end_a, side_half, whole_b, end_half, grads_out_b
    )
    far_end_a = move(end_a, middle)
    end_b = move(whole_b, inward)
    side_end_half = flip(end_half, 2)
    side_grads_b = flip(grads_out_b, 2)
    far_a, far_b = by_y(far_u0, far_u1, wide_a), by_y(far_u0, far_u1, wide_b)
    out_a = move(far_a, outward)
    side_all = gather_chips(side_half)

    own, end = [(0, d) for d in range(4)], [(1, d) for d in range(4)]
    rows_in = [tokens, core_tokens, tokens, end_all]

    (held_b,) = ffn(
        clock,
        1,
        [(whole_b, 0), (far_b, 2)],
        rows_in,
        [group(own[:2] + end[:2], (0, 1))],
        [],
        None,
        None,
        [],
        "b_first",
    )
    (held_a,) = ffn(
        clock,
        1,
        [(whole_a, 0), (end_a, 1), (far_a, 2)],
        [tokens, core_tokens],
        [group(own[:2], (0, 1, 2))],
        [],
        None,
        None,
        [],
        "a_first",
    )
    held_a, held_b, side_all, end_all, side_end_half, side_grads_b, *moved = wait(
        held_a,
        held_b,
        side_all,
        end_all,
        side_end_half,
        side_grads_b,
        grads_out_a[0],
        grads_out_a[1],
        far_end_a,
        end_b,
        out_a,
    )
    *grads_out_a, far_end_a, end_b, out_a = moved
    far_end_b = move(end_b, middle)
    out_end_a = move(far_end_a, outward)
    side_grads_a = [flip(grads_out_a[0], 2), flip(grads_out_a[1], 3)]
    side_end_all = gather_chips(side_end_half)
    pieces = [grads[0][:, chunk_b], core_grads[:, chunk_b], side_grads_b[0]]
    own_grads_b = jnp.concatenate([*pieces, flip(side_grads_b[1], 1)], axis=0)
    end_grads_b = move(own_grads_b, inward)
    rows_in = [tokens, core_tokens, side_all, end_all, end_all]
    blocks_b = [(whole_b, 0), (end_b, 1), (far_b, 2)]
    (held_b,) = ffn(
        clock,
        1,
        blocks_b,
        rows_in,
        [group(own[:2] + end[:2], (1,), True), group(own[2:], (0, 1, 2))],
        [held_b],
        None,
        None,
        [],
        "b_next",
    )
    blocks_a = [(whole_a, 0), (end_a, 1), (far_a, 2)]
    (held_late,) = ffn(
        clock, 1, blocks_a, rows_in[:3], [group(own[2:], (0, 1, 2))], [], None, None, [], "a_second"
    )
    held_b, held_late, *side_grads_a = wait(held_b, held_late, *side_grads_a)
    grads_a = [(grads[0], 0, 0), (core_grads, 0, 0)] + [(piece, 0, 0) for piece in side_grads_a]
    sums = ffn(
        clock,
        1,
        [(far_end_a, 3)],
        rows_in[:3],
        [group(own, (0,), True)],
        [held_a, held_late],
        grads_a,
        proj_a,
        [],
        "a_inner",
    )
    sums[0], side_end_all, out_end_a = wait(sums[0], side_end_all, out_end_a)
    rows_in[4] = side_end_all

    def ends_a(*values):
        so_far, index, grads_a, rows_a, blocks = values[0], values[1], values[2:6], values[6:9], values[9:]
        blocks = [(value, plane) for plane, value in enumerate(blocks)]
        grads_a = [(piece, 0, 0) for piece in grads_a]
        units = [group(own, (0, 1, 2, 3))]
        return ffn(index, 0, blocks, rows_a, units, [], grads_a, proj_a, [so_far], "a_end")[0]

    values = [sums[0], clock, *(piece for piece, _, _ in grads_a), *rows_in[:3]]
    values += [whole_a, end_a, out_a, out_end_a]
    sums = [lax.cond(inner == 1, lambda *values: values[0], ends_a, *values)]
    sums[0], end_grads_b, far_end_b = wait(sums[0], end_grads_b, far_end_b)
    grads_b = [(value, d * rows, 0) for value in (own_grads_b, end_grads_b) for d in range(4)]
    sums = ffn(
        clock,
        1,
        [*blocks_b, (far_end_b, 3)],
        rows_in,
        [group(own, (3,), True), group(end[:2], (3,), True), group(end[2:], (0, 1, 2, 3))],
        [held_b],
        grads_b,
        proj_b,
        sums,
        "b_last",
        order=(0, 1, 4, 5, 2, 3),
    )

    kept = jnp.stack([part[d] for part in sums for d in (0, 2)])
    sent = jnp.stack([part[d] for part in sums for d in (1, 3)])
    kept = kept + flip(sent, 1)
    keep = lax.dynamic_slice_in_dim(kept, x * ranks, ranks, 1)
    give = lax.dynamic_slice_in_dim(kept, (1 - x) * ranks, ranks, 1)
    send = give.astype(jnp.bfloat16)
    both_ways = [
        (2 * i + t, 2 * (i ^ 2) + 1 - t) for i in range(16) for t in range(2)
    ]
    arrived = [
        across(send[0::2]),
        flip(keep[1::2].astype(jnp.bfloat16), 2),
        lax.ppermute(send[1::2], ("dp", "tensor"), both_ways),
    ]
    total = keep[0::2]
    for value in arrived:
        total = total + value.astype(jnp.float32)
    back = move(total[1].astype(jnp.bfloat16), outward)

    docs = doc_lengths.shape[0]
    gate_out, up_out = pl.pallas_call(
        functools.partial(features_kernel, docs),
        out_shape=[jax.ShapeDtypeStruct((docs, share, ranks), jnp.float32)] * 2,
        in_specs=[vmem_spec()] * 3 + [smem_spec()],
        out_specs=[vmem_spec()] * 2,
        name="features",
    )(total[0], back, projected, doc_lengths)
    return jnp.swapaxes(gate_out, 1, 2), jnp.swapaxes(up_out, 1, 2)


def solution(mesh):
    placed = (
        P("dp", None),
        P("dp"),
        P("dp", "tensor"),
        P("dp", "tensor"),
        P("dp", "tensor"),
        P(),
        P(None, "tensor"),
        P(None, "tensor"),
    )
    planes = mesh.shape["dp"] == 16 and mesh.shape["tensor"] == 2
    return jax.shard_map(
        shards_planes if planes else shards_any,
        mesh=mesh,
        in_specs=placed,
        out_specs=(P("dp", None, "tensor"), P("dp", None, "tensor")),
        check_vma=False,
    )
```

```python
import functools

import jax
import jax.numpy as jnp
from jax import lax
from jax.experimental import pallas as pl
from jax.experimental.pallas import tpu as pltpu
from jax.sharding import PartitionSpec as P

DOC_LEN = 192
VMEM_LIMIT = 46 * 1024 * 1024
UNITS = 7
UNITS_A = 3


def contract_last(left, right):
    return lax.dot_general(
        left, right, (((1,), (1,)), ((), ())), preferred_element_type=jnp.float32
    )


def per_document(inputs, side):
    docs = inputs.shape[0] // DOC_LEN
    left = inputs.reshape(docs, DOC_LEN, inputs.shape[1])
    right = side.reshape(docs, DOC_LEN, side.shape[1])
    return 0.0625 * jnp.einsum("ntr,nts->nrs", left, right, preferred_element_type=jnp.float32)


def shards_any(
    tokens,
    doc_lengths,
    gate_weight,
    up_weight,
    hidden_grad,
    in_projector,
    gate_projector,
    up_projector,
):
    def add_one(piece):
        return jnp.dot(tokens, piece, preferred_element_type=jnp.float32)

    gate = add_one(lax.all_gather(gate_weight, "dp", axis=0, tiled=True))
    up = add_one(lax.all_gather(up_weight, "dp", axis=0, tiled=True))
    sig = jax.nn.sigmoid(gate)
    cotangent = hidden_grad.astype(jnp.float32)
    grad_gate = (cotangent * up * sig * (1.0 + gate * (1.0 - sig))).astype(jnp.bfloat16)
    grad_up = (cotangent * gate * sig).astype(jnp.bfloat16)
    rows = tokens.shape[0]
    within = jnp.arange(rows, dtype=jnp.int32) % DOC_LEN
    limits = jnp.repeat(doc_lengths, DOC_LEN)
    mask = (within < limits).astype(jnp.bfloat16)
    projected = contract_last(tokens, in_projector)
    inputs = projected.astype(jnp.bfloat16) * mask[:, None]
    gate_part = contract_last(grad_gate, gate_projector)
    up_part = contract_last(grad_up, up_projector)
    gate_full, up_full = lax.psum((gate_part, up_part), "tensor")
    share = gate_full.shape[1] // lax.axis_size("tensor")
    start = lax.axis_index("tensor") * share
    gate_sum = lax.dynamic_slice_in_dim(gate_full, start, share, 1)
    up_sum = lax.dynamic_slice_in_dim(up_full, start, share, 1)
    gate_side = gate_sum.astype(jnp.bfloat16)
    up_side = up_sum.astype(jnp.bfloat16)
    return (per_document(inputs, gate_side), per_document(inputs, up_side))


def vmem_spec():
    return pl.BlockSpec(memory_space=pltpu.VMEM)


def hbm_spec():
    return pl.BlockSpec(memory_space=pltpu.HBM)


def smem_spec():
    return pl.BlockSpec(memory_space=pltpu.SMEM)


def ffn_kernel(cfg, idx, *refs):
    refs = list(refs)
    groups, final = cfg["groups"], cfg["final"]
    block_refs = [refs.pop(0) for _ in range(cfg["n_blocks"])]
    token_refs = [refs.pop(0) for _ in range(cfg["n_tokens"])]
    held = [refs.pop(0) for _ in cfg["held"]]
    if final:
        grad_refs = [refs.pop(0) for _ in cfg["grads"]]
        gate_proj, up_proj = refs.pop(0), refs.pop(0)
    prev = [refs.pop(0) for _ in range(cfg["prev"])]
    outs = [refs.pop(0) for _ in range(cfg["n_outs"])]
    block_buffer, block_sem = refs.pop(0), refs.pop(0)
    token_buffers = [(refs.pop(0), refs.pop(0)) for _ in groups]
    if held:
        held_buffer, held_sem = refs.pop(0), refs.pop(0)
    if final:
        grad_buffer, grad_sem = refs
    else:
        out_buffer, out_sem = refs
    core = idx[0]
    deep, width, rows = cfg["deep"], cfg["width"], cfg["rows"]

    def token_copy(buffer, sem, r, i, unit, at):
        g, d = unit
        ref, z = token_refs[cfg["tokens"][g][d]], idx[1 + cfg["planes"][at]]
        if len(ref.shape) == 2:
            source = ref.at[:, pl.ds(pl.multiple_of(z * deep, deep), deep)]
        else:
            start = pl.multiple_of((z % 2) * deep, deep)
            source = ref.at[2 * (core ^ (d & 1)) + z // 2, :, pl.ds(start, deep)]
        return pltpu.make_async_copy(source, buffer.at[r, :, pl.ds(i * deep, deep)], sem.at[r, i])

    def block_copy(at):
        target = block_buffer.at[pl.ds(at * deep, deep)]
        return pltpu.make_async_copy(block_refs[at], target, block_sem.at[at])

    def arrived(buffer, sem, slot):
        pltpu.make_async_copy(buffer.at[slot], buffer.at[slot], sem.at[slot]).wait()

    def out_copy(n):
        return pltpu.make_async_copy(out_buffer.at[n % 2], outs[0].at[n], out_sem.at[n % 2])

    kept = [ref.at[i] for ref, count in zip(held, cfg["held"]) for i in range(count)]
    kept = [kept[i] for i in cfg["order"]]

    def grad_copy(n, unit):
        ref, (row, column) = grad_refs[4 * unit[0] + unit[1]], cfg["grads"][4 * unit[0] + unit[1]]
        source = ref.at[pl.ds(row, rows), pl.ds(column, width)]
        return pltpu.make_async_copy(source, grad_buffer.at[n], grad_sem.at[n])

    def finish(group, r, n, gate, up):
        s, d = group["units"][0]
        d = d + r
        arrived(grad_buffer, grad_sem, n)
        sig = 1.0 / (1.0 + jnp.exp(-gate))
        cotangent = grad_buffer[n].astype(jnp.float32)
        grad_gate = (cotangent * up * sig * (1.0 + gate * (1.0 - sig))).astype(jnp.bfloat16)
        grad_up = (cotangent * gate * sig).astype(jnp.bfloat16)
        part = contract_last(gate_proj[...], grad_gate)
        part += contract_last(up_proj[...], grad_up)
        outs[s][d] = prev[s][d] + part if s < len(prev) else part

    def work():
        n_kept, n, asked = 0, 0, set()
        for group, (buffer, sem) in zip(groups, token_buffers):
            for r, unit in enumerate(group["units"]):
                for i, at in enumerate(group["blocks"]):
                    if at not in asked:
                        asked.add(at)
                        block_copy(at).start()
                    token_copy(buffer, sem, r, i, unit, at).start()
                if group["held"]:
                    pltpu.make_async_copy(
                        kept[n_kept], held_buffer.at[n_kept], held_sem.at[n_kept]
                    ).start()
                    n_kept += 1
                if final:
                    grad_copy(n, unit).start()
                n += 1
        n_kept, first, here = 0, 0, set()
        for group, (buffer, sem) in zip(groups, token_buffers):
            size, count = len(group["blocks"]), len(group["units"])
            fresh = [at for at in group["blocks"] if at not in here]
            here.update(fresh)
            planes = slice(group["blocks"][0] * deep, (group["blocks"][0] + size) * deep)
            for at in fresh:
                block_copy(at).wait()

            def unit_step(
                r, carry, group=group, buffer=buffer, sem=sem, planes=planes, n_kept=n_kept, first=first
            ):
                for i in range(buffer.shape[2] // deep):
                    target = buffer.at[r, :, pl.ds(i * deep, deep)]
                    pltpu.make_async_copy(target, target, sem.at[r, i]).wait()
                pair = [
                    jnp.dot(
                        buffer[r],
                        block_buffer[planes, h * width : (h + 1) * width],
                        preferred_element_type=jnp.float32,
                    )
                    for h in (0, 1)
                ]
                if group["held"]:
                    arrived(held_buffer, held_sem, n_kept + r)
                    pair = [
                        value + held_buffer[n_kept + r, :, h * width : (h + 1) * width].astype(jnp.float32)
                        for h, value in enumerate(pair)
                    ]
                n = first + r
                if final:
                    finish(group, r, n, *pair)
                else:

                    @pl.when(n >= 2)
                    def _():
                        out_copy(n - 2).wait()

                    for h, value in enumerate(pair):
                        out_buffer[n % 2, :, h * width : (h + 1) * width] = value.astype(out_buffer.dtype)
                    out_copy(n).start()
                return carry

            lax.fori_loop(0, count, unit_step, 0)
            first += count
            if group["held"]:
                n_kept += count
        if not final:
            out_copy(first - 2).wait()
            out_copy(first - 1).wait()

    runs = idx[5] == cfg["inner"]
    pl.when(runs)(work)

    if final:

        @pl.when(jnp.logical_not(runs))
        def _():
            for s, out in enumerate(outs):
                out[...] = prev[s][...] if s < len(prev) else jnp.zeros_like(out)


TOKENS = ((0, 1, 2, 2), (3, 3, 4, 4))


def group(units, blocks, held=False):
    return {"units": units, "blocks": blocks, "held": held}


def ffn(idx, inner, blocks, tokens, groups, held, grads, proj, prev, name, order=None):
    deep, width = blocks[0][0].shape[0], blocks[0][0].shape[1] // 2
    rows = tokens[0].shape[-2]
    final = grads is not None
    n_units = sum(len(one["units"]) for one in groups)
    cfg = {
        "inner": inner,
        "planes": [plane for _, plane in blocks],
        "tokens": TOKENS,
        "n_blocks": len(blocks),
        "n_tokens": len(tokens),
        "groups": groups,
        "held": [value.shape[0] for value in held],
        "order": order or range(sum(value.shape[0] for value in held)),
        "grads": [place for _, *place in grads or ()],
        "final": final,
        "n_outs": len(grads) // 4 if final else 1,
        "prev": len(prev),
        "deep": deep,
        "width": width,
        "rows": rows,
    }
    large = [*(block for block, _ in blocks), *tokens, *held, *(one[0] for one in grads or ())]
    args = [pltpu.with_memory_space_constraint(value, pltpu.HBM) for value in large]
    specs = [hbm_spec()] * len(args)
    args += [*(proj if final else ()), *prev]
    specs += [vmem_spec()] * (len(args) - len(specs))
    if final:
        shapes = [(4, proj[0].shape[0], rows)] * (len(grads) // 4)
    else:
        shapes = [(n_units, rows, 2 * width)]
    if final:
        results = [jax.ShapeDtypeStruct(shape, jnp.float32) for shape in shapes]
    else:
        results = [pltpu.HBM(shape, jnp.bfloat16) for shape in shapes]

    def buffers(count, shape, dtype):
        return [pltpu.VMEM((count, rows, shape), dtype), pltpu.SemaphoreType.DMA((count,))]

    scratch = [
        pltpu.VMEM((len(blocks) * deep, 2 * width), jnp.bfloat16),
        pltpu.SemaphoreType.DMA((len(blocks),)),
    ]
    for one in groups:
        units, size = len(one["units"]), len(one["blocks"])
        scratch.append(pltpu.VMEM((units, rows, size * deep), jnp.bfloat16))
        scratch.append(pltpu.SemaphoreType.DMA((units, size)))
    if held:
        scratch += buffers(sum(cfg["held"]), 2 * width, jnp.bfloat16)
    if final:
        scratch += buffers(n_units, width, jnp.bfloat16)
    else:
        scratch += buffers(2, 2 * width, jnp.bfloat16)
    parts = pl.pallas_call(
        functools.partial(ffn_kernel, cfg),
        out_shape=results,
        in_specs=[smem_spec()] + specs,
        out_specs=[vmem_spec() if final else hbm_spec()] * len(shapes),
        scratch_shapes=scratch,
        compiler_params=pltpu.CompilerParams(vmem_limit_bytes=VMEM_LIMIT),
        cost_estimate=pl.CostEstimate(flops=1, bytes_accessed=1, transcendentals=0),
        name=name,
    )(idx, *args)
    return list(parts)


def features_kernel(docs, mine, sent, projected, limits, gate_out, up_out):
    side = (mine[...] + sent[...].astype(jnp.float32)).astype(jnp.bfloat16)
    share = side.shape[0] // 2
    inputs = projected[...].astype(jnp.bfloat16)
    position = lax.broadcasted_iota(jnp.int32, inputs.shape, 1)
    for n in range(docs):
        within = position - n * DOC_LEN
        used = jnp.logical_and(within >= 0, within < limits[n])
        left = jnp.where(used, inputs, jnp.zeros_like(inputs))
        gate_out[n] = 0.0625 * contract_last(side[:share], left)
        up_out[n] = 0.0625 * contract_last(side[share:], left)


def shards_planes(
    tokens,
    doc_lengths,
    gate_weight,
    up_weight,
    hidden_grad,
    in_projector,
    gate_projector,
    up_projector,
):
    dp, x = lax.axis_index("dp"), lax.axis_index("tensor")
    z, q = dp // 4, dp % 4
    inner = jnp.logical_or(z == 1, z == 2).astype(jnp.int32)
    first_pair = z < 2
    far_inner = jnp.where(first_pair, 2, 1)
    far_outer = jnp.where(first_pair, 3, 0)
    y, core = (dp // 2) % 2, dp % 2
    idx = jnp.stack([core, z, z ^ 1, far_inner, far_outer, inner]).astype(jnp.int32)

    def planes(pairs):
        return [(4 * a + i, 4 * b + i) for a, b in pairs for i in range(4)]

    inward, outward = planes([(0, 1), (3, 2)]), planes([(1, 0), (2, 3)])
    middle, neighbours = planes([(1, 2), (2, 1)]), planes([(0, 1), (1, 0), (2, 3), (3, 2)])

    def move(value, perm):
        return lax.ppermute(value, "dp", perm)

    def flip(value, d):
        return lax.ppermute(value, "dp", [(i, i ^ d) for i in range(16)])

    def across(value):
        return lax.ppermute(value, "tensor", [(0, 1), (1, 0)])

    def gather_chips(value):
        groups = [[4 * pair + i for i in range(4)] for pair in range(8)]
        return lax.all_gather(value, ("dp", "tensor"), axis_index_groups=groups)

    rows, model = tokens.shape
    depth, hidden = gate_weight.shape
    quarter = hidden // 4
    cut = quarter // UNITS * UNITS_A
    chunk_a, chunk_b = slice(0, cut), slice(cut, quarter)
    ranks = gate_projector.shape[0]
    share = ranks // 2

    clock = idx

    def wait(*values):
        nonlocal clock
        *values, clock = lax.optimization_barrier((*values, clock))
        return values[0] if len(values) == 1 else values

    def quarter_of(value, d):
        return lax.dynamic_slice_in_dim(value, (q ^ d) * quarter, quarter, 1)

    def weights_for(d, chunk):
        gate, up = quarter_of(gate_weight, d), quarter_of(up_weight, d)
        return jnp.concatenate([gate[:, chunk], up[:, chunk]], axis=1)

    def grads_for(d, chunk):
        return quarter_of(hidden_grad, d)[:, chunk]

    def by_core(mine, other):
        first, second = jnp.where(core == 0, mine, other), jnp.where(core == 0, other, mine)
        return jnp.concatenate([first, second], axis=0)

    def by_y(mine, other, columns):
        mine, other = mine[:, columns], other[:, columns]
        first, second = jnp.where(y == 0, mine, other), jnp.where(y == 0, other, mine)
        return jnp.concatenate([first, second], axis=0)

    gate_mine = lax.dynamic_slice_in_dim(gate_projector, q * quarter, quarter, 1)
    up_mine = lax.dynamic_slice_in_dim(up_projector, q * quarter, quarter, 1)
    nothing = jnp.zeros((share, quarter), jnp.bfloat16)
    gate_rows = jnp.concatenate([gate_mine[:share], nothing, gate_mine[share:], nothing], axis=0)
    up_rows = jnp.concatenate([nothing, up_mine[:share], nothing, up_mine[share:]], axis=0)
    proj_a = [gate_rows[:, chunk_a], up_rows[:, chunk_a]]
    proj_b = [gate_rows[:, chunk_b], up_rows[:, chunk_b]]

    wide_a, wide_b = slice(0, 2 * cut), slice(2 * cut, 2 * quarter)
    both = [
        jnp.concatenate([weights_for(d, chunk_a), weights_for(d, chunk_b)], axis=1) for d in range(4)
    ]
    half = lax.dynamic_slice_in_dim(tokens, x * (model // 2), model // 2, 1)
    core_in = flip(both[1], 1)
    both[2], both[3], half, core_in = wait(both[2], both[3], half, core_in)
    side_in, cross_in = flip(both[2], 2), flip(both[3], 3)
    end_half = move(half, inward)
    u0 = by_core(both[0], core_in)
    far_u0 = move(u0, middle)
    core_tokens = flip(tokens, 1)
    grads = [quarter_of(hidden_grad, d) for d in range(4)]
    grads_out_a = [piece[:, chunk_a] for piece in grads[2:]]
    grads_out_b = jnp.stack([piece[:, chunk_b] for piece in grads[2:]])
    core_grads = flip(grads[1], 1)
    projected = contract_last(in_projector, tokens)

    side_in, cross_in, far_u0, end_half, half, core_tokens, projected = wait(
        side_in, cross_in, far_u0, end_half, half, core_tokens, projected
    )
    grads_out_a[0], grads_out_a[1], grads_out_b, core_grads, grads[0] = wait(
        *grads_out_a, grads_out_b, core_grads, grads[0]
    )
    proj_a[0], proj_a[1], proj_b[0], proj_b[1] = wait(*proj_a, *proj_b)
    u1 = by_core(side_in, cross_in)
    far_u1 = move(u1, middle)
    whole_a = by_y(u0, u1, wide_a)
    end_a = move(whole_a, neighbours)
    side_half = flip(half, 2)
    end_all = gather_chips(end_half)
    whole_b = by_y(u0, u1, wide_b)

    far_u1, end_a, side_half, whole_b, end_half, grads_out_b = wait(
        far_u1, end_a, side_half, whole_b, end_half, grads_out_b
    )
    far_end_a = move(end_a, middle)
    end_b = move(whole_b, inward)
    side_end_half = flip(end_half, 2)
    side_grads_b = flip(grads_out_b, 2)
    far_a, far_b = by_y(far_u0, far_u1, wide_a), by_y(far_u0, far_u1, wide_b)
    out_a = move(far_a, outward)
    side_all = gather_chips(side_half)

    own, end = [(0, d) for d in range(4)], [(1, d) for d in range(4)]
    rows_in = [tokens, core_tokens, tokens, end_all]

    (held_b,) = ffn(
        clock,
        1,
        [(whole_b, 0), (far_b, 2)],
        rows_in,
        [group(own[:2] + end[:2], (0, 1))],
        [],
        None,
        None,
        [],
        "b_first",
    )
    (held_a,) = ffn(
        clock,
        1,
        [(whole_a, 0), (end_a, 1), (far_a, 2)],
        [tokens, core_tokens],
        [group(own[:2], (0, 1, 2))],
        [],
        None,
        None,
        [],
        "a_first",
    )
    held_a, held_b, side_all, end_all, side_end_half, side_grads_b, *moved = wait(
        held_a,
        held_b,
        side_all,
        end_all,
        side_end_half,
        side_grads_b,
        grads_out_a[0],
        grads_out_a[1],
        far_end_a,
        end_b,
        out_a,
    )
    *grads_out_a, far_end_a, end_b, out_a = moved
    far_end_b = move(end_b, middle)
    out_end_a = move(far_end_a, outward)
    side_grads_a = [flip(grads_out_a[0], 2), flip(grads_out_a[1], 3)]
    side_end_all = gather_chips(side_end_half)
    pieces = [grads[0][:, chunk_b], core_grads[:, chunk_b], side_grads_b[0]]
    own_grads_b = jnp.concatenate([*pieces, flip(side_grads_b[1], 1)], axis=0)
    end_grads_b = move(own_grads_b, inward)
    rows_in = [tokens, core_tokens, side_all, end_all, end_all]
    blocks_b = [(whole_b, 0), (end_b, 1), (far_b, 2)]
    (held_b,) = ffn(
        clock,
        1,
        blocks_b,
        rows_in,
        [group(own[:2] + end[:2], (1,), True), group(own[2:], (0, 1, 2))],
        [held_b],
        None,
        None,
        [],
        "b_next",
    )
    blocks_a = [(whole_a, 0), (end_a, 1), (far_a, 2)]
    (held_late,) = ffn(
        clock, 1, blocks_a, rows_in[:3], [group(own[2:], (0, 1, 2))], [], None, None, [], "a_second"
    )
    held_b, held_late, *side_grads_a = wait(held_b, held_late, *side_grads_a)
    grads_a = [(grads[0], 0, 0), (core_grads, 0, 0)] + [(piece, 0, 0) for piece in side_grads_a]
    sums = ffn(
        clock,
        1,
        [(far_end_a, 3)],
        rows_in[:3],
        [group(own, (0,), True)],
        [held_a, held_late],
        grads_a,
        proj_a,
        [],
        "a_inner",
    )
    sums[0], side_end_all, out_end_a = wait(sums[0], side_end_all, out_end_a)
    rows_in[4] = side_end_all

    def ends_a(*values):
        so_far, index, grads_a, rows_a, blocks = values[0], values[1], values[2:6], values[6:9], values[9:]
        blocks = [(value, plane) for plane, value in enumerate(blocks)]
        grads_a = [(piece, 0, 0) for piece in grads_a]
        units = [group(own, (0, 1, 2, 3))]
        return ffn(index, 0, blocks, rows_a, units, [], grads_a, proj_a, [so_far], "a_end")[0]

    values = [sums[0], clock, *(piece for piece, _, _ in grads_a), *rows_in[:3]]
    values += [whole_a, end_a, out_a, out_end_a]
    sums = [lax.cond(inner == 1, lambda *values: values[0], ends_a, *values)]
    sums[0], end_grads_b, far_end_b = wait(sums[0], end_grads_b, far_end_b)
    grads_b = [(value, d * rows, 0) for value in (own_grads_b, end_grads_b) for d in range(4)]
    sums = ffn(
        clock,
        1,
        [*blocks_b, (far_end_b, 3)],
        rows_in,
        [group(own, (3,), True), group(end[:2], (3,), True), group(end[2:], (0, 1, 2, 3))],
        [held_b],
        grads_b,
        proj_b,
        sums,
        "b_last",
        order=(0, 1, 4, 5, 2, 3),
    )

    kept = jnp.stack([part[d] for part in sums for d in (0, 2)])
    sent = jnp.stack([part[d] for part in sums for d in (1, 3)])
    kept = kept + flip(sent, 1)
    keep = lax.dynamic_slice_in_dim(kept, x * ranks, ranks, 1)
    give = lax.dynamic_slice_in_dim(kept, (1 - x) * ranks, ranks, 1)
    send = give.astype(jnp.bfloat16)
    both_ways = [
        (2 * i + t, 2 * (i ^ 2) + 1 - t) for i in range(16) for t in range(2)
    ]
    arrived = [
        across(send[0::2]),
        flip(keep[1::2].astype(jnp.bfloat16), 2),
        lax.ppermute(send[1::2], ("dp", "tensor"), both_ways),
    ]
    total = keep[0::2]
    for value in arrived:
        total = total + value.astype(jnp.float32)
    back = move(total[1].astype(jnp.bfloat16), outward)

    docs = doc_lengths.shape[0]
    gate_out, up_out = pl.pallas_call(
        functools.partial(features_kernel, docs),
        out_shape=[jax.ShapeDtypeStruct((docs, share, ranks), jnp.float32)] * 2,
        in_specs=[vmem_spec()] * 3 + [smem_spec()],
        out_specs=[vmem_spec()] * 2,
        name="features",
    )(total[0], back, projected, doc_lengths)
    return jnp.swapaxes(gate_out, 1, 2), jnp.swapaxes(up_out, 1, 2)


def solution(mesh):
    placed = (
        P("dp", None),
        P("dp"),
        P("dp", "tensor"),
        P("dp", "tensor"),
        P("dp", "tensor"),
        P(),
        P(None, "tensor"),
        P(None, "tensor"),
    )
    planes = mesh.shape["dp"] == 16 and mesh.shape["tensor"] == 2
    return jax.shard_map(
        shards_planes if planes else shards_any,
        mesh=mesh,
        in_specs=placed,
        out_specs=(P("dp", None, "tensor"), P("dp", None, "tensor")),
        check_vma=False,
    )
```

```python
import functools

import jax
import jax.numpy as jnp
from jax import lax
from jax.experimental import pallas as pl
from jax.experimental.pallas import tpu as pltpu
from jax.sharding import PartitionSpec as P

DOC_LEN = 192
VMEM_LIMIT = 46 * 1024 * 1024
UNITS = 7
UNITS_A = 3


def contract_last(left, right):
    return lax.dot_general(
        left, right, (((1,), (1,)), ((), ())), preferred_element_type=jnp.float32
    )


def per_document(inputs, side):
    docs = inputs.shape[0] // DOC_LEN
    left = inputs.reshape(docs, DOC_LEN, inputs.shape[1])
    right = side.reshape(docs, DOC_LEN, side.shape[1])
    return 0.0625 * jnp.einsum("ntr,nts->nrs", left, right, preferred_element_type=jnp.float32)


def shards_any(
    tokens,
    doc_lengths,
    gate_weight,
    up_weight,
    hidden_grad,
    in_projector,
    gate_projector,
    up_projector,
):
    def add_one(piece):
        return jnp.dot(tokens, piece, preferred_element_type=jnp.float32)

    gate = add_one(lax.all_gather(gate_weight, "dp", axis=0, tiled=True))
    up = add_one(lax.all_gather(up_weight, "dp", axis=0, tiled=True))
    sig = jax.nn.sigmoid(gate)
    cotangent = hidden_grad.astype(jnp.float32)
    grad_gate = (cotangent * up * sig * (1.0 + gate * (1.0 - sig))).astype(jnp.bfloat16)
    grad_up = (cotangent * gate * sig).astype(jnp.bfloat16)
    rows = tokens.shape[0]
    within = jnp.arange(rows, dtype=jnp.int32) % DOC_LEN
    limits = jnp.repeat(doc_lengths, DOC_LEN)
    mask = (within < limits).astype(jnp.bfloat16)
    projected = contract_last(tokens, in_projector)
    inputs = projected.astype(jnp.bfloat16) * mask[:, None]
    gate_part = contract_last(grad_gate, gate_projector)
    up_part = contract_last(grad_up, up_projector)
    gate_full, up_full = lax.psum((gate_part, up_part), "tensor")
    share = gate_full.shape[1] // lax.axis_size("tensor")
    start = lax.axis_index("tensor") * share
    gate_sum = lax.dynamic_slice_in_dim(gate_full, start, share, 1)
    up_sum = lax.dynamic_slice_in_dim(up_full, start, share, 1)
    gate_side = gate_sum.astype(jnp.bfloat16)
    up_side = up_sum.astype(jnp.bfloat16)
    return (per_document(inputs, gate_side), per_document(inputs, up_side))


def vmem_spec():
    return pl.BlockSpec(memory_space=pltpu.VMEM)


def hbm_spec():
    return pl.BlockSpec(memory_space=pltpu.HBM)


def smem_spec():
    return pl.BlockSpec(memory_space=pltpu.SMEM)


def ffn_kernel(cfg, idx, *refs):
    refs = list(refs)
    groups, final = cfg["groups"], cfg["final"]
    block_refs = [refs.pop(0) for _ in range(cfg["n_blocks"])]
    token_refs = [refs.pop(0) for _ in range(cfg["n_tokens"])]
    held = [refs.pop(0) for _ in cfg["held"]]
    if final:
        grad_refs = [refs.pop(0) for _ in cfg["grads"]]
        gate_proj, up_proj = refs.pop(0), refs.pop(0)
    prev = [refs.pop(0) for _ in range(cfg["prev"])]
    outs = [refs.pop(0) for _ in range(cfg["n_outs"])]
    block_buffer, block_sem = refs.pop(0), refs.pop(0)
    token_buffers = [(refs.pop(0), refs.pop(0)) for _ in groups]
    if held:
        held_buffer, held_sem = refs.pop(0), refs.pop(0)
    if final:
        grad_buffer, grad_sem = refs
    else:
        out_buffer, out_sem = refs
    core = idx[0]
    deep, width, rows = cfg["deep"], cfg["width"], cfg["rows"]

    def token_copy(buffer, sem, r, i, unit, at):
        g, d = unit
        ref, z = token_refs[cfg["tokens"][g][d]], idx[1 + cfg["planes"][at]]
        if len(ref.shape) == 2:
            source = ref.at[:, pl.ds(pl.multiple_of(z * deep, deep), deep)]
        else:
            start = pl.multiple_of((z % 2) * deep, deep)
            source = ref.at[2 * (core ^ (d & 1)) + z // 2, :, pl.ds(start, deep)]
        return pltpu.make_async_copy(source, buffer.at[r, :, pl.ds(i * deep, deep)], sem.at[r, i])

    def block_copy(at):
        target = block_buffer.at[pl.ds(at * deep, deep)]
        return pltpu.make_async_copy(block_refs[at], target, block_sem.at[at])

    def arrived(buffer, sem, slot):
        pltpu.make_async_copy(buffer.at[slot], buffer.at[slot], sem.at[slot]).wait()

    def out_copy(n):
        return pltpu.make_async_copy(out_buffer.at[n % 2], outs[0].at[n], out_sem.at[n % 2])

    kept = [ref.at[i] for ref, count in zip(held, cfg["held"]) for i in range(count)]
    kept = [kept[i] for i in cfg["order"]]

    def grad_copy(n, unit):
        ref, (row, column) = grad_refs[4 * unit[0] + unit[1]], cfg["grads"][4 * unit[0] + unit[1]]
        source = ref.at[pl.ds(row, rows), pl.ds(column, width)]
        return pltpu.make_async_copy(source, grad_buffer.at[n], grad_sem.at[n])

    def finish(group, r, n, gate, up):
        s, d = group["units"][0]
        d = d + r
        arrived(grad_buffer, grad_sem, n)
        sig = 1.0 / (1.0 + jnp.exp(-gate))
        cotangent = grad_buffer[n].astype(jnp.float32)
        grad_gate = (cotangent * up * sig * (1.0 + gate * (1.0 - sig))).astype(jnp.bfloat16)
        grad_up = (cotangent * gate * sig).astype(jnp.bfloat16)
        part = contract_last(gate_proj[...], grad_gate)
        part += contract_last(up_proj[...], grad_up)
        outs[s][d] = prev[s][d] + part if s < len(prev) else part

    def work():
        n_kept, n, asked = 0, 0, set()
        for group, (buffer, sem) in zip(groups, token_buffers):
            for r, unit in enumerate(group["units"]):
                for i, at in enumerate(group["blocks"]):
                    if at not in asked:
                        asked.add(at)
                        block_copy(at).start()
                    token_copy(buffer, sem, r, i, unit, at).start()
                if group["held"]:
                    pltpu.make_async_copy(
                        kept[n_kept], held_buffer.at[n_kept], held_sem.at[n_kept]
                    ).start()
                    n_kept += 1
                if final:
                    grad_copy(n, unit).start()
                n += 1
        n_kept, first, here = 0, 0, set()
        for group, (buffer, sem) in zip(groups, token_buffers):
            size, count = len(group["blocks"]), len(group["units"])
            fresh = [at for at in group["blocks"] if at not in here]
            here.update(fresh)
            planes = slice(group["blocks"][0] * deep, (group["blocks"][0] + size) * deep)
            for at in fresh:
                block_copy(at).wait()

            def unit_step(
                r, carry, group=group, buffer=buffer, sem=sem, planes=planes, n_kept=n_kept, first=first
            ):
                for i in range(buffer.shape[2] // deep):
                    target = buffer.at[r, :, pl.ds(i * deep, deep)]
                    pltpu.make_async_copy(target, target, sem.at[r, i]).wait()
                pair = [
                    jnp.dot(
                        buffer[r],
                        block_buffer[planes, h * width : (h + 1) * width],
                        preferred_element_type=jnp.float32,
                    )
                    for h in (0, 1)
                ]
                if group["held"]:
                    arrived(held_buffer, held_sem, n_kept + r)
                    pair = [
                        value + held_buffer[n_kept + r, :, h * width : (h + 1) * width].astype(jnp.float32)
                        for h, value in enumerate(pair)
                    ]
                n = first + r
                if final:
                    finish(group, r, n, *pair)
                else:

                    @pl.when(n >= 2)
                    def _():
                        out_copy(n - 2).wait()

                    for h, value in enumerate(pair):
                        out_buffer[n % 2, :, h * width : (h + 1) * width] = value.astype(out_buffer.dtype)
                    out_copy(n).start()
                return carry

            lax.fori_loop(0, count, unit_step, 0)
            first += count
            if group["held"]:
                n_kept += count
        if not final:
            out_copy(first - 2).wait()
            out_copy(first - 1).wait()

    runs = idx[5] == cfg["inner"]
    pl.when(runs)(work)

    if final:

        @pl.when(jnp.logical_not(runs))
        def _():
            for s, out in enumerate(outs):
                out[...] = prev[s][...] if s < len(prev) else jnp.zeros_like(out)


TOKENS = ((0, 1, 2, 2), (3, 3, 4, 4))


def group(units, blocks, held=False):
    return {"units": units, "blocks": blocks, "held": held}


def ffn(idx, inner, blocks, tokens, groups, held, grads, proj, prev, name, order=None):
    deep, width = blocks[0][0].shape[0], blocks[0][0].shape[1] // 2
    rows = tokens[0].shape[-2]
    final = grads is not None
    n_units = sum(len(one["units"]) for one in groups)
    cfg = {
        "inner": inner,
        "planes": [plane for _, plane in blocks],
        "tokens": TOKENS,
        "n_blocks": len(blocks),
        "n_tokens": len(tokens),
        "groups": groups,
        "held": [value.shape[0] for value in held],
        "order": order or range(sum(value.shape[0] for value in held)),
        "grads": [place for _, *place in grads or ()],
        "final": final,
        "n_outs": len(grads) // 4 if final else 1,
        "prev": len(prev),
        "deep": deep,
        "width": width,
        "rows": rows,
    }
    large = [*(block for block, _ in blocks), *tokens, *held, *(one[0] for one in grads or ())]
    args = [pltpu.with_memory_space_constraint(value, pltpu.HBM) for value in large]
    specs = [hbm_spec()] * len(args)
    args += [*(proj if final else ()), *prev]
    specs += [vmem_spec()] * (len(args) - len(specs))
    if final:
        shapes = [(4, proj[0].shape[0], rows)] * (len(grads) // 4)
    else:
        shapes = [(n_units, rows, 2 * width)]
    if final:
        results = [jax.ShapeDtypeStruct(shape, jnp.float32) for shape in shapes]
    else:
        results = [pltpu.HBM(shape, jnp.bfloat16) for shape in shapes]

    def buffers(count, shape, dtype):
        return [pltpu.VMEM((count, rows, shape), dtype), pltpu.SemaphoreType.DMA((count,))]

    scratch = [
        pltpu.VMEM((len(blocks) * deep, 2 * width), jnp.bfloat16),
        pltpu.SemaphoreType.DMA((len(blocks),)),
    ]
    for one in groups:
        units, size = len(one["units"]), len(one["blocks"])
        scratch.append(pltpu.VMEM((units, rows, size * deep), jnp.bfloat16))
        scratch.append(pltpu.SemaphoreType.DMA((units, size)))
    if held:
        scratch += buffers(sum(cfg["held"]), 2 * width, jnp.bfloat16)
    if final:
        scratch += buffers(n_units, width, jnp.bfloat16)
    else:
        scratch += buffers(2, 2 * width, jnp.bfloat16)
    parts = pl.pallas_call(
        functools.partial(ffn_kernel, cfg),
        out_shape=results,
        in_specs=[smem_spec()] + specs,
        out_specs=[vmem_spec() if final else hbm_spec()] * len(shapes),
        scratch_shapes=scratch,
        compiler_params=pltpu.CompilerParams(vmem_limit_bytes=VMEM_LIMIT),
        cost_estimate=pl.CostEstimate(flops=1, bytes_accessed=1, transcendentals=0),
        name=name,
    )(idx, *args)
    return list(parts)


def features_kernel(docs, mine, sent, projected, limits, gate_out, up_out):
    side = (mine[...] + sent[...].astype(jnp.float32)).astype(jnp.bfloat16)
    share = side.shape[0] // 2
    inputs = projected[...].astype(jnp.bfloat16)
    position = lax.broadcasted_iota(jnp.int32, inputs.shape, 1)
    for n in range(docs):
        within = position - n * DOC_LEN
        used = jnp.logical_and(within >= 0, within < limits[n])
        left = jnp.where(used, inputs, jnp.zeros_like(inputs))
        gate_out[n] = 0.0625 * contract_last(side[:share], left)
        up_out[n] = 0.0625 * contract_last(side[share:], left)


def shards_planes(
    tokens,
    doc_lengths,
    gate_weight,
    up_weight,
    hidden_grad,
    in_projector,
    gate_projector,
    up_projector,
):
    dp, x = lax.axis_index("dp"), lax.axis_index("tensor")
    z, q = dp // 4, dp % 4
    inner = jnp.logical_or(z == 1, z == 2).astype(jnp.int32)
    first_pair = z < 2
    far_inner = jnp.where(first_pair, 2, 1)
    far_outer = jnp.where(first_pair, 3, 0)
    y, core = (dp // 2) % 2, dp % 2
    idx = jnp.stack([core, z, z ^ 1, far_inner, far_outer, inner]).astype(jnp.int32)

    def planes(pairs):
        return [(4 * a + i, 4 * b + i) for a, b in pairs for i in range(4)]

    inward, outward = planes([(0, 1), (3, 2)]), planes([(1, 0), (2, 3)])
    middle, neighbours = planes([(1, 2), (2, 1)]), planes([(0, 1), (1, 0), (2, 3), (3, 2)])

    def move(value, perm):
        return lax.ppermute(value, "dp", perm)

    def flip(value, d):
        return lax.ppermute(value, "dp", [(i, i ^ d) for i in range(16)])

    def across(value):
        return lax.ppermute(value, "tensor", [(0, 1), (1, 0)])

    def gather_chips(value):
        groups = [[4 * pair + i for i in range(4)] for pair in range(8)]
        return lax.all_gather(value, ("dp", "tensor"), axis_index_groups=groups)

    rows, model = tokens.shape
    depth, hidden = gate_weight.shape
    quarter = hidden // 4
    cut = quarter // UNITS * UNITS_A
    chunk_a, chunk_b = slice(0, cut), slice(cut, quarter)
    ranks = gate_projector.shape[0]
    share = ranks // 2

    clock = idx

    def wait(*values):
        nonlocal clock
        *values, clock = lax.optimization_barrier((*values, clock))
        return values[0] if len(values) == 1 else values

    def quarter_of(value, d):
        return lax.dynamic_slice_in_dim(value, (q ^ d) * quarter, quarter, 1)

    def weights_for(d, whole_gate, whole_up):
        gate, up = quarter_of(whole_gate, d), quarter_of(whole_up, d)
        pieces = [value[:, chunk] for chunk in (chunk_a, chunk_b) for value in (gate, up)]
        return jnp.concatenate(pieces, axis=1)

    def grads_for(d, chunk):
        return quarter_of(hidden_grad, d)[:, chunk]

    def by_core(mine, other):
        first, second = jnp.where(core == 0, mine, other), jnp.where(core == 0, other, mine)
        return jnp.concatenate([first, second], axis=0)

    def by_y(mine, other, columns):
        mine, other = mine[:, columns], other[:, columns]
        first, second = jnp.where(y == 0, mine, other), jnp.where(y == 0, other, mine)
        return jnp.concatenate([first, second], axis=0)

    gate_mine = lax.dynamic_slice_in_dim(gate_projector, q * quarter, quarter, 1)
    up_mine = lax.dynamic_slice_in_dim(up_projector, q * quarter, quarter, 1)
    nothing = jnp.zeros((share, quarter), jnp.bfloat16)
    gate_rows = jnp.concatenate([gate_mine[:share], nothing, gate_mine[share:], nothing], axis=0)
    up_rows = jnp.concatenate([nothing, up_mine[:share], nothing, up_mine[share:]], axis=0)
    proj_a = [gate_rows[:, chunk_a], up_rows[:, chunk_a]]
    proj_b = [gate_rows[:, chunk_b], up_rows[:, chunk_b]]

    wide_a, wide_b = slice(0, 2 * cut), slice(2 * cut, 2 * quarter)
    to_core = weights_for(1, gate_weight, up_weight)
    weights = lax.optimization_barrier((gate_weight, up_weight, to_core))
    both = [None if d == 1 else weights_for(d, *weights[:2]) for d in range(4)]
    both[1] = weights[2]
    half = lax.dynamic_slice_in_dim(tokens, x * (model // 2), model // 2, 1)
    core_in = flip(both[1], 1)
    half, core_in = wait(half, core_in)
    side_in, cross_in = flip(both[2], 2), flip(both[3], 3)
    end_half = move(half, inward)
    u0 = by_core(both[0], core_in)
    far_u0 = move(u0, middle)
    core_tokens = flip(tokens, 1)
    grads = [quarter_of(hidden_grad, d) for d in range(4)]
    grads_out_a = [piece[:, chunk_a] for piece in grads[2:]]
    grads_out_b = jnp.stack([piece[:, chunk_b] for piece in grads[2:]])
    core_grads = flip(grads[1], 1)
    projected = contract_last(in_projector, tokens)

    side_in, cross_in, far_u0, end_half, half, core_tokens, projected = wait(
        side_in, cross_in, far_u0, end_half, half, core_tokens, projected
    )
    grads_out_a[0], grads_out_a[1], grads_out_b, core_grads, grads[0] = wait(
        *grads_out_a, grads_out_b, core_grads, grads[0]
    )
    proj_a[0], proj_a[1], proj_b[0], proj_b[1] = wait(*proj_a, *proj_b)
    u1 = by_core(side_in, cross_in)
    far_u1 = move(u1, middle)
    whole_a = by_y(u0, u1, wide_a)
    end_a = move(whole_a, neighbours)
    side_half = flip(half, 2)
    end_all = gather_chips(end_half)
    whole_b = by_y(u0, u1, wide_b)

    far_u1, end_a, side_half, whole_b, end_half, grads_out_b = wait(
        far_u1, end_a, side_half, whole_b, end_half, grads_out_b
    )
    far_end_a = move(end_a, middle)
    end_b = move(whole_b, inward)
    side_end_half = flip(end_half, 2)
    side_grads_b = flip(grads_out_b, 2)
    far_a, far_b = by_y(far_u0, far_u1, wide_a), by_y(far_u0, far_u1, wide_b)
    out_a = move(far_a, outward)
    side_all = gather_chips(side_half)

    own, end = [(0, d) for d in range(4)], [(1, d) for d in range(4)]
    rows_in = [tokens, core_tokens, tokens, end_all]

    (held_b,) = ffn(
        clock,
        1,
        [(whole_b, 0), (far_b, 2)],
        rows_in,
        [group(own[:2] + end[:2], (0, 1))],
        [],
        None,
        None,
        [],
        "b_first",
    )
    (held_a,) = ffn(
        clock,
        1,
        [(whole_a, 0), (end_a, 1), (far_a, 2)],
        [tokens, core_tokens],
        [group(own[:2], (0, 1, 2))],
        [],
        None,
        None,
        [],
        "a_first",
    )
    held_a, held_b, side_all, end_all, side_end_half, side_grads_b, *moved = wait(
        held_a,
        held_b,
        side_all,
        end_all,
        side_end_half,
        side_grads_b,
        grads_out_a[0],
        grads_out_a[1],
        far_end_a,
        end_b,
        out_a,
    )
    *grads_out_a, far_end_a, end_b, out_a = moved
    far_end_b = move(end_b, middle)
    out_end_a = move(far_end_a, outward)
    side_grads_a = [flip(grads_out_a[0], 2), flip(grads_out_a[1], 3)]
    side_end_all = gather_chips(side_end_half)
    pieces = [grads[0][:, chunk_b], core_grads[:, chunk_b], side_grads_b[0]]
    own_grads_b = jnp.concatenate([*pieces, flip(side_grads_b[1], 1)], axis=0)
    end_grads_b = move(own_grads_b, inward)
    rows_in = [tokens, core_tokens, side_all, end_all, end_all]
    blocks_b = [(whole_b, 0), (end_b, 1), (far_b, 2)]
    (held_b,) = ffn(
        clock,
        1,
        blocks_b,
        rows_in,
        [group(own[:2] + end[:2], (1,), True), group(own[2:], (0, 1, 2))],
        [held_b],
        None,
        None,
        [],
        "b_next",
    )
    blocks_a = [(whole_a, 0), (end_a, 1), (far_a, 2)]
    (held_late,) = ffn(
        clock, 1, blocks_a, rows_in[:3], [group(own[2:], (0, 1, 2))], [], None, None, [], "a_second"
    )
    held_b, held_late, *side_grads_a = wait(held_b, held_late, *side_grads_a)
    grads_a = [(grads[0], 0, 0), (core_grads, 0, 0)] + [(piece, 0, 0) for piece in side_grads_a]
    sums = ffn(
        clock,
        1,
        [(far_end_a, 3)],
        rows_in[:3],
        [group(own, (0,), True)],
        [held_a, held_late],
        grads_a,
        proj_a,
        [],
        "a_inner",
    )
    sums[0], side_end_all, out_end_a = wait(sums[0], side_end_all, out_end_a)
    rows_in[4] = side_end_all

    def ends_a(*values):
        so_far, index, grads_a, rows_a, blocks = values[0], values[1], values[2:6], values[6:9], values[9:]
        blocks = [(value, plane) for plane, value in enumerate(blocks)]
        grads_a = [(piece, 0, 0) for piece in grads_a]
        units = [group(own, (0, 1, 2, 3))]
        return ffn(index, 0, blocks, rows_a, units, [], grads_a, proj_a, [so_far], "a_end")[0]

    values = [sums[0], clock, *(piece for piece, _, _ in grads_a), *rows_in[:3]]
    values += [whole_a, end_a, out_a, out_end_a]
    sums = [lax.cond(inner == 1, lambda *values: values[0], ends_a, *values)]
    sums[0], end_grads_b, far_end_b = wait(sums[0], end_grads_b, far_end_b)
    grads_b = [(value, d * rows, 0) for value in (own_grads_b, end_grads_b) for d in range(4)]
    sums = ffn(
        clock,
        1,
        [*blocks_b, (far_end_b, 3)],
        rows_in,
        [group(own, (3,), True), group(end[:2], (3,), True), group(end[2:], (0, 1, 2, 3))],
        [held_b],
        grads_b,
        proj_b,
        sums,
        "b_last",
        order=(0, 1, 4, 5, 2, 3),
    )

    kept = jnp.stack([part[d] for part in sums for d in (0, 2)])
    sent = jnp.stack([part[d] for part in sums for d in (1, 3)])
    kept = kept + flip(sent, 1)
    keep = lax.dynamic_slice_in_dim(kept, x * ranks, ranks, 1)
    give = lax.dynamic_slice_in_dim(kept, (1 - x) * ranks, ranks, 1)
    send = give.astype(jnp.bfloat16)
    both_ways = [
        (2 * i + t, 2 * (i ^ 2) + 1 - t) for i in range(16) for t in range(2)
    ]
    arrived = [
        across(send[0::2]),
        flip(keep[1::2].astype(jnp.bfloat16), 2),
        lax.ppermute(send[1::2], ("dp", "tensor"), both_ways),
    ]
    total = keep[0::2]
    for value in arrived:
        total = total + value.astype(jnp.float32)
    back = move(total[1].astype(jnp.bfloat16), outward)

    docs = doc_lengths.shape[0]
    gate_out, up_out = pl.pallas_call(
        functools.partial(features_kernel, docs),
        out_shape=[jax.ShapeDtypeStruct((docs, share, ranks), jnp.float32)] * 2,
        in_specs=[vmem_spec()] * 3 + [smem_spec()],
        out_specs=[vmem_spec()] * 2,
        name="features",
    )(total[0], back, projected, doc_lengths)
    return jnp.swapaxes(gate_out, 1, 2), jnp.swapaxes(up_out, 1, 2)


def solution(mesh):
    placed = (
        P("dp", None),
        P("dp"),
        P("dp", "tensor"),
        P("dp", "tensor"),
        P("dp", "tensor"),
        P(),
        P(None, "tensor"),
        P(None, "tensor"),
    )
    planes = mesh.shape["dp"] == 16 and mesh.shape["tensor"] == 2
    return jax.shard_map(
        shards_planes if planes else shards_any,
        mesh=mesh,
        in_specs=placed,
        out_specs=(P("dp", None, "tensor"), P("dp", None, "tensor")),
        check_vma=False,
    )
```

```python
import functools

import jax
import jax.numpy as jnp
from jax import lax
from jax.experimental import pallas as pl
from jax.experimental.pallas import tpu as pltpu
from jax.sharding import PartitionSpec as P

DOC_LEN = 192
VMEM_LIMIT = 46 * 1024 * 1024
UNITS = 7
UNITS_A = 3


def contract_last(left, right):
    return lax.dot_general(
        left, right, (((1,), (1,)), ((), ())), preferred_element_type=jnp.float32
    )


def per_document(inputs, side):
    docs = inputs.shape[0] // DOC_LEN
    left = inputs.reshape(docs, DOC_LEN, inputs.shape[1])
    right = side.reshape(docs, DOC_LEN, side.shape[1])
    return 0.0625 * jnp.einsum("ntr,nts->nrs", left, right, preferred_element_type=jnp.float32)


def shards_any(
    tokens,
    doc_lengths,
    gate_weight,
    up_weight,
    hidden_grad,
    in_projector,
    gate_projector,
    up_projector,
):
    def add_one(piece):
        return jnp.dot(tokens, piece, preferred_element_type=jnp.float32)

    gate = add_one(lax.all_gather(gate_weight, "dp", axis=0, tiled=True))
    up = add_one(lax.all_gather(up_weight, "dp", axis=0, tiled=True))
    sig = jax.nn.sigmoid(gate)
    cotangent = hidden_grad.astype(jnp.float32)
    grad_gate = (cotangent * up * sig * (1.0 + gate * (1.0 - sig))).astype(jnp.bfloat16)
    grad_up = (cotangent * gate * sig).astype(jnp.bfloat16)
    rows = tokens.shape[0]
    within = jnp.arange(rows, dtype=jnp.int32) % DOC_LEN
    limits = jnp.repeat(doc_lengths, DOC_LEN)
    mask = (within < limits).astype(jnp.bfloat16)
    projected = contract_last(tokens, in_projector)
    inputs = projected.astype(jnp.bfloat16) * mask[:, None]
    gate_part = contract_last(grad_gate, gate_projector)
    up_part = contract_last(grad_up, up_projector)
    gate_full, up_full = lax.psum((gate_part, up_part), "tensor")
    share = gate_full.shape[1] // lax.axis_size("tensor")
    start = lax.axis_index("tensor") * share
    gate_sum = lax.dynamic_slice_in_dim(gate_full, start, share, 1)
    up_sum = lax.dynamic_slice_in_dim(up_full, start, share, 1)
    gate_side = gate_sum.astype(jnp.bfloat16)
    up_side = up_sum.astype(jnp.bfloat16)
    return (per_document(inputs, gate_side), per_document(inputs, up_side))


def vmem_spec():
    return pl.BlockSpec(memory_space=pltpu.VMEM)


def hbm_spec():
    return pl.BlockSpec(memory_space=pltpu.HBM)


def smem_spec():
    return pl.BlockSpec(memory_space=pltpu.SMEM)


def ffn_kernel(cfg, idx, *refs):
    refs = list(refs)
    groups, final = cfg["groups"], cfg["final"]
    block_refs = [refs.pop(0) for _ in range(cfg["n_blocks"])]
    token_refs = [refs.pop(0) for _ in range(cfg["n_tokens"])]
    held = [refs.pop(0) for _ in cfg["held"]]
    if final:
        grad_refs = [refs.pop(0) for _ in cfg["grads"]]
        gate_proj, up_proj = refs.pop(0), refs.pop(0)
    prev = [refs.pop(0) for _ in range(cfg["prev"])]
    outs = [refs.pop(0) for _ in range(cfg["n_outs"])]
    block_buffer, block_sem = refs.pop(0), refs.pop(0)
    token_buffers = [(refs.pop(0), refs.pop(0)) for _ in groups]
    if held:
        held_buffer, held_sem = refs.pop(0), refs.pop(0)
    if final:
        grad_buffer, grad_sem = refs
    else:
        out_buffer, out_sem = refs
    core = idx[0]
    deep, width, rows = cfg["deep"], cfg["width"], cfg["rows"]

    def token_copy(buffer, sem, r, i, unit, at):
        g, d = unit
        ref, z = token_refs[cfg["tokens"][g][d]], idx[1 + cfg["planes"][at]]
        if len(ref.shape) == 2:
            source = ref.at[:, pl.ds(pl.multiple_of(z * deep, deep), deep)]
        else:
            start = pl.multiple_of((z % 2) * deep, deep)
            source = ref.at[2 * (core ^ (d & 1)) + z // 2, :, pl.ds(start, deep)]
        return pltpu.make_async_copy(source, buffer.at[r, :, pl.ds(i * deep, deep)], sem.at[r, i])

    def block_copy(at):
        target = block_buffer.at[pl.ds(at * deep, deep)]
        return pltpu.make_async_copy(block_refs[at], target, block_sem.at[at])

    def arrived(buffer, sem, slot):
        pltpu.make_async_copy(buffer.at[slot], buffer.at[slot], sem.at[slot]).wait()

    def out_copy(n):
        return pltpu.make_async_copy(out_buffer.at[n % 2], outs[0].at[n], out_sem.at[n % 2])

    kept = [ref.at[i] for ref, count in zip(held, cfg["held"]) for i in range(count)]
    kept = [kept[i] for i in cfg["order"]]

    def grad_copy(n, unit):
        ref, (row, column) = grad_refs[4 * unit[0] + unit[1]], cfg["grads"][4 * unit[0] + unit[1]]
        source = ref.at[pl.ds(row, rows), pl.ds(column, width)]
        return pltpu.make_async_copy(source, grad_buffer.at[n], grad_sem.at[n])

    def finish(group, r, n, gate, up):
        s, d = group["units"][0]
        d = d + r
        arrived(grad_buffer, grad_sem, n)
        sig = 0.5 * jnp.tanh(0.5 * gate) + 0.5
        cotangent = grad_buffer[n].astype(jnp.float32)
        grad_gate = (cotangent * up * sig * (1.0 + gate * (1.0 - sig))).astype(jnp.bfloat16)
        grad_up = (cotangent * gate * sig).astype(jnp.bfloat16)
        part = contract_last(gate_proj[...], grad_gate)
        part += contract_last(up_proj[...], grad_up)
        outs[s][d] = prev[s][d] + part if s < len(prev) else part

    def work():
        n_kept, n, asked = 0, 0, set()
        for group, (buffer, sem) in zip(groups, token_buffers):
            for r, unit in enumerate(group["units"]):
                for i, at in enumerate(group["blocks"]):
                    if at not in asked:
                        asked.add(at)
                        block_copy(at).start()
                    token_copy(buffer, sem, r, i, unit, at).start()
                if group["held"]:
                    pltpu.make_async_copy(
                        kept[n_kept], held_buffer.at[n_kept], held_sem.at[n_kept]
                    ).start()
                    n_kept += 1
                if final:
                    grad_copy(n, unit).start()
                n += 1
        n_kept, first, here = 0, 0, set()
        for group, (buffer, sem) in zip(groups, token_buffers):
            size, count = len(group["blocks"]), len(group["units"])
            fresh = [at for at in group["blocks"] if at not in here]
            here.update(fresh)
            planes = slice(group["blocks"][0] * deep, (group["blocks"][0] + size) * deep)
            for at in fresh:
                block_copy(at).wait()

            def unit_step(
                r, carry, group=group, buffer=buffer, sem=sem, planes=planes, n_kept=n_kept, first=first
            ):
                for i in range(buffer.shape[2] // deep):
                    target = buffer.at[r, :, pl.ds(i * deep, deep)]
                    pltpu.make_async_copy(target, target, sem.at[r, i]).wait()
                pair = [
                    jnp.dot(
                        buffer[r],
                        block_buffer[planes, h * width : (h + 1) * width],
                        preferred_element_type=jnp.float32,
                    )
                    for h in (0, 1)
                ]
                if group["held"]:
                    arrived(held_buffer, held_sem, n_kept + r)
                    pair = [
                        value + held_buffer[n_kept + r, :, h * width : (h + 1) * width].astype(jnp.float32)
                        for h, value in enumerate(pair)
                    ]
                n = first + r
                if final:
                    finish(group, r, n, *pair)
                else:

                    @pl.when(n >= 2)
                    def _():
                        out_copy(n - 2).wait()

                    for h, value in enumerate(pair):
                        out_buffer[n % 2, :, h * width : (h + 1) * width] = value.astype(out_buffer.dtype)
                    out_copy(n).start()
                return carry

            lax.fori_loop(0, count, unit_step, 0)
            first += count
            if group["held"]:
                n_kept += count
        if not final:
            out_copy(first - 2).wait()
            out_copy(first - 1).wait()

    runs = idx[5] == cfg["inner"]
    pl.when(runs)(work)

    if final:

        @pl.when(jnp.logical_not(runs))
        def _():
            for s, out in enumerate(outs):
                out[...] = prev[s][...] if s < len(prev) else jnp.zeros_like(out)


TOKENS = ((0, 1, 2, 2), (3, 3, 4, 4))


def group(units, blocks, held=False):
    return {"units": units, "blocks": blocks, "held": held}


def ffn(idx, inner, blocks, tokens, groups, held, grads, proj, prev, name, order=None):
    deep, width = blocks[0][0].shape[0], blocks[0][0].shape[1] // 2
    rows = tokens[0].shape[-2]
    final = grads is not None
    n_units = sum(len(one["units"]) for one in groups)
    cfg = {
        "inner": inner,
        "planes": [plane for _, plane in blocks],
        "tokens": TOKENS,
        "n_blocks": len(blocks),
        "n_tokens": len(tokens),
        "groups": groups,
        "held": [value.shape[0] for value in held],
        "order": order or range(sum(value.shape[0] for value in held)),
        "grads": [place for _, *place in grads or ()],
        "final": final,
        "n_outs": len(grads) // 4 if final else 1,
        "prev": len(prev),
        "deep": deep,
        "width": width,
        "rows": rows,
    }
    large = [*(block for block, _ in blocks), *tokens, *held, *(one[0] for one in grads or ())]
    args = [pltpu.with_memory_space_constraint(value, pltpu.HBM) for value in large]
    specs = [hbm_spec()] * len(args)
    args += [*(proj if final else ()), *prev]
    specs += [vmem_spec()] * (len(args) - len(specs))
    if final:
        shapes = [(4, proj[0].shape[0], rows)] * (len(grads) // 4)
    else:
        shapes = [(n_units, rows, 2 * width)]
    if final:
        results = [jax.ShapeDtypeStruct(shape, jnp.float32) for shape in shapes]
    else:
        results = [pltpu.HBM(shape, jnp.bfloat16) for shape in shapes]

    def buffers(count, shape, dtype):
        return [pltpu.VMEM((count, rows, shape), dtype), pltpu.SemaphoreType.DMA((count,))]

    scratch = [
        pltpu.VMEM((len(blocks) * deep, 2 * width), jnp.bfloat16),
        pltpu.SemaphoreType.DMA((len(blocks),)),
    ]
    for one in groups:
        units, size = len(one["units"]), len(one["blocks"])
        scratch.append(pltpu.VMEM((units, rows, size * deep), jnp.bfloat16))
        scratch.append(pltpu.SemaphoreType.DMA((units, size)))
    if held:
        scratch += buffers(sum(cfg["held"]), 2 * width, jnp.bfloat16)
    if final:
        scratch += buffers(n_units, width, jnp.bfloat16)
    else:
        scratch += buffers(2, 2 * width, jnp.bfloat16)
    parts = pl.pallas_call(
        functools.partial(ffn_kernel, cfg),
        out_shape=results,
        in_specs=[smem_spec()] + specs,
        out_specs=[vmem_spec() if final else hbm_spec()] * len(shapes),
        scratch_shapes=scratch,
        compiler_params=pltpu.CompilerParams(vmem_limit_bytes=VMEM_LIMIT),
        cost_estimate=pl.CostEstimate(flops=1, bytes_accessed=1, transcendentals=0),
        name=name,
    )(idx, *args)
    return list(parts)


def features_kernel(docs, mine, sent, projected, limits, gate_out, up_out):
    side = (mine[...] + sent[...].astype(jnp.float32)).astype(jnp.bfloat16)
    share = side.shape[0] // 2
    inputs = projected[...].astype(jnp.bfloat16)
    position = lax.broadcasted_iota(jnp.int32, inputs.shape, 1)
    for n in range(docs):
        within = position - n * DOC_LEN
        used = jnp.logical_and(within >= 0, within < limits[n])
        left = jnp.where(used, inputs, jnp.zeros_like(inputs))
        gate_out[n] = 0.0625 * contract_last(side[:share], left)
        up_out[n] = 0.0625 * contract_last(side[share:], left)


def shards_planes(
    tokens,
    doc_lengths,
    gate_weight,
    up_weight,
    hidden_grad,
    in_projector,
    gate_projector,
    up_projector,
):
    dp, x = lax.axis_index("dp"), lax.axis_index("tensor")
    z, q = dp // 4, dp % 4
    inner = jnp.logical_or(z == 1, z == 2).astype(jnp.int32)
    first_pair = z < 2
    far_inner = jnp.where(first_pair, 2, 1)
    far_outer = jnp.where(first_pair, 3, 0)
    y, core = (dp // 2) % 2, dp % 2
    idx = jnp.stack([core, z, z ^ 1, far_inner, far_outer, inner]).astype(jnp.int32)

    def planes(pairs):
        return [(4 * a + i, 4 * b + i) for a, b in pairs for i in range(4)]

    inward, outward = planes([(0, 1), (3, 2)]), planes([(1, 0), (2, 3)])
    middle, neighbours = planes([(1, 2), (2, 1)]), planes([(0, 1), (1, 0), (2, 3), (3, 2)])

    def move(value, perm):
        return lax.ppermute(value, "dp", perm)

    def flip(value, d):
        return lax.ppermute(value, "dp", [(i, i ^ d) for i in range(16)])

    def across(value):
        return lax.ppermute(value, "tensor", [(0, 1), (1, 0)])

    def gather_chips(value):
        groups = [[4 * pair + i for i in range(4)] for pair in range(8)]
        return lax.all_gather(value, ("dp", "tensor"), axis_index_groups=groups)

    rows, model = tokens.shape
    depth, hidden = gate_weight.shape
    quarter = hidden // 4
    cut = quarter // UNITS * UNITS_A
    chunk_a, chunk_b = slice(0, cut), slice(cut, quarter)
    ranks = gate_projector.shape[0]
    share = ranks // 2

    clock = idx

    def wait(*values):
        nonlocal clock
        *values, clock = lax.optimization_barrier((*values, clock))
        return values[0] if len(values) == 1 else values

    def quarter_of(value, d):
        return lax.dynamic_slice_in_dim(value, (q ^ d) * quarter, quarter, 1)

    def weights_for(d, whole_gate, whole_up):
        gate, up = quarter_of(whole_gate, d), quarter_of(whole_up, d)
        pieces = [value[:, chunk] for chunk in (chunk_a, chunk_b) for value in (gate, up)]
        return jnp.concatenate(pieces, axis=1)

    def grads_for(d, chunk):
        return quarter_of(hidden_grad, d)[:, chunk]

    def by_core(mine, other):
        first, second = jnp.where(core == 0, mine, other), jnp.where(core == 0, other, mine)
        return jnp.concatenate([first, second], axis=0)

    def by_y(mine, other, columns):
        mine, other = mine[:, columns], other[:, columns]
        first, second = jnp.where(y == 0, mine, other), jnp.where(y == 0, other, mine)
        return jnp.concatenate([first, second], axis=0)

    gate_mine = lax.dynamic_slice_in_dim(gate_projector, q * quarter, quarter, 1)
    up_mine = lax.dynamic_slice_in_dim(up_projector, q * quarter, quarter, 1)
    nothing = jnp.zeros((share, quarter), jnp.bfloat16)
    gate_rows = jnp.concatenate([gate_mine[:share], nothing, gate_mine[share:], nothing], axis=0)
    up_rows = jnp.concatenate([nothing, up_mine[:share], nothing, up_mine[share:]], axis=0)
    proj_a = [gate_rows[:, chunk_a], up_rows[:, chunk_a]]
    proj_b = [gate_rows[:, chunk_b], up_rows[:, chunk_b]]

    wide_a, wide_b = slice(0, 2 * cut), slice(2 * cut, 2 * quarter)
    to_core = weights_for(1, gate_weight, up_weight)
    weights = lax.optimization_barrier((gate_weight, up_weight, to_core))
    both = [None if d == 1 else weights_for(d, *weights[:2]) for d in range(4)]
    both[1] = weights[2]
    half = lax.dynamic_slice_in_dim(tokens, x * (model // 2), model // 2, 1)
    core_in = flip(both[1], 1)
    half, core_in = wait(half, core_in)
    side_in, cross_in = flip(both[2], 2), flip(both[3], 3)
    end_half = move(half, inward)
    u0 = by_core(both[0], core_in)
    far_u0 = move(u0, middle)
    core_tokens = flip(tokens, 1)
    grads = [quarter_of(hidden_grad, d) for d in range(4)]
    grads_out_a = [piece[:, chunk_a] for piece in grads[2:]]
    grads_out_b = jnp.stack([piece[:, chunk_b] for piece in grads[2:]])
    core_grads = flip(grads[1], 1)
    projected = contract_last(in_projector, tokens)

    side_in, cross_in, far_u0, end_half, half, core_tokens, projected = wait(
        side_in, cross_in, far_u0, end_half, half, core_tokens, projected
    )
    grads_out_a[0], grads_out_a[1], grads_out_b, core_grads, grads[0] = wait(
        *grads_out_a, grads_out_b, core_grads, grads[0]
    )
    proj_a[0], proj_a[1], proj_b[0], proj_b[1] = wait(*proj_a, *proj_b)
    u1 = by_core(side_in, cross_in)
    far_u1 = move(u1, middle)
    whole_a = by_y(u0, u1, wide_a)
    end_a = move(whole_a, neighbours)
    side_half = flip(half, 2)
    end_all = gather_chips(end_half)
    whole_b = by_y(u0, u1, wide_b)

    far_u1, end_a, side_half, whole_b, end_half, grads_out_b = wait(
        far_u1, end_a, side_half, whole_b, end_half, grads_out_b
    )
    far_end_a = move(end_a, middle)
    end_b = move(whole_b, inward)
    side_end_half = flip(end_half, 2)
    side_grads_b = flip(grads_out_b, 2)
    far_a, far_b = by_y(far_u0, far_u1, wide_a), by_y(far_u0, far_u1, wide_b)
    out_a = move(far_a, outward)
    side_all = gather_chips(side_half)

    own, end = [(0, d) for d in range(4)], [(1, d) for d in range(4)]
    rows_in = [tokens, core_tokens, tokens, end_all]

    (held_b,) = ffn(
        clock,
        1,
        [(whole_b, 0), (far_b, 2)],
        rows_in,
        [group(own[:2] + end[:2], (0, 1))],
        [],
        None,
        None,
        [],
        "b_first",
    )
    (held_a,) = ffn(
        clock,
        1,
        [(whole_a, 0), (end_a, 1), (far_a, 2)],
        [tokens, core_tokens],
        [group(own[:2], (0, 1, 2))],
        [],
        None,
        None,
        [],
        "a_first",
    )
    held_a, held_b, side_all, end_all, side_end_half, side_grads_b, *moved = wait(
        held_a,
        held_b,
        side_all,
        end_all,
        side_end_half,
        side_grads_b,
        grads_out_a[0],
        grads_out_a[1],
        far_end_a,
        end_b,
        out_a,
    )
    *grads_out_a, far_end_a, end_b, out_a = moved
    far_end_b = move(end_b, middle)
    out_end_a = move(far_end_a, outward)
    side_grads_a = [flip(grads_out_a[0], 2), flip(grads_out_a[1], 3)]
    side_end_all = gather_chips(side_end_half)
    pieces = [grads[0][:, chunk_b], core_grads[:, chunk_b], side_grads_b[0]]
    own_grads_b = jnp.concatenate([*pieces, flip(side_grads_b[1], 1)], axis=0)
    end_grads_b = move(own_grads_b, inward)
    rows_in = [tokens, core_tokens, side_all, end_all, end_all]
    blocks_b = [(whole_b, 0), (end_b, 1), (far_b, 2)]
    (held_b,) = ffn(
        clock,
        1,
        blocks_b,
        rows_in,
        [group(own[:2] + end[:2], (1,), True), group(own[2:], (0, 1, 2))],
        [held_b],
        None,
        None,
        [],
        "b_next",
    )
    blocks_a = [(whole_a, 0), (end_a, 1), (far_a, 2)]
    held_b, *side_grads_a = wait(held_b, *side_grads_a)
    grads_a = [(grads[0], 0, 0), (core_grads, 0, 0)] + [(piece, 0, 0) for piece in side_grads_a]
    sums = ffn(
        clock,
        1,
        [*blocks_a, (far_end_a, 3)],
        rows_in[:3],
        [group(own[:2], (3,), True), group(own[2:], (0, 1, 2, 3))],
        [held_a],
        grads_a,
        proj_a,
        [],
        "a_inner",
    )
    sums[0], side_end_all, out_end_a = wait(sums[0], side_end_all, out_end_a)
    rows_in[4] = side_end_all

    def ends_a(*values):
        so_far, index, grads_a, rows_a, blocks = values[0], values[1], values[2:6], values[6:9], values[9:]
        blocks = [(value, plane) for plane, value in enumerate(blocks)]
        grads_a = [(piece, 0, 0) for piece in grads_a]
        units = [group(own, (0, 1, 2, 3))]
        return ffn(index, 0, blocks, rows_a, units, [], grads_a, proj_a, [so_far], "a_end")[0]

    values = [sums[0], clock, *(piece for piece, _, _ in grads_a), *rows_in[:3]]
    values += [whole_a, end_a, out_a, out_end_a]
    sums = [lax.cond(inner == 1, lambda *values: values[0], ends_a, *values)]
    sums[0], end_grads_b, far_end_b = wait(sums[0], end_grads_b, far_end_b)
    grads_b = [(value, d * rows, 0) for value in (own_grads_b, end_grads_b) for d in range(4)]
    sums = ffn(
        clock,
        1,
        [*blocks_b, (far_end_b, 3)],
        rows_in,
        [group(own, (3,), True), group(end[:2], (3,), True), group(end[2:], (0, 1, 2, 3))],
        [held_b],
        grads_b,
        proj_b,
        sums,
        "b_last",
        order=(0, 1, 4, 5, 2, 3),
    )

    kept = jnp.stack([part[d] for part in sums for d in (0, 2)])
    sent = jnp.stack([part[d] for part in sums for d in (1, 3)])
    kept = kept + flip(sent.astype(jnp.bfloat16), 1).astype(jnp.float32)
    keep = lax.dynamic_slice_in_dim(kept, x * ranks, ranks, 1)
    give = lax.dynamic_slice_in_dim(kept, (1 - x) * ranks, ranks, 1)
    send = give.astype(jnp.bfloat16)
    both_ways = [
        (2 * i + t, 2 * (i ^ 2) + 1 - t) for i in range(16) for t in range(2)
    ]
    arrived = [
        across(send[0::2]),
        flip(keep[1::2].astype(jnp.bfloat16), 2),
        lax.ppermute(send[1::2], ("dp", "tensor"), both_ways),
    ]
    total = keep[0::2]
    for value in arrived:
        total = total + value.astype(jnp.float32)
    back = move(total[1].astype(jnp.bfloat16), outward)

    docs = doc_lengths.shape[0]
    gate_out, up_out = pl.pallas_call(
        functools.partial(features_kernel, docs),
        out_shape=[jax.ShapeDtypeStruct((docs, share, ranks), jnp.float32)] * 2,
        in_specs=[vmem_spec()] * 3 + [smem_spec()],
        out_specs=[vmem_spec()] * 2,
        name="features",
    )(total[0], back, projected, doc_lengths)
    return jnp.swapaxes(gate_out, 1, 2), jnp.swapaxes(up_out, 1, 2)


def solution(mesh):
    placed = (
        P("dp", None),
        P("dp"),
        P("dp", "tensor"),
        P("dp", "tensor"),
        P("dp", "tensor"),
        P(),
        P(None, "tensor"),
        P(None, "tensor"),
    )
    planes = mesh.shape["dp"] == 16 and mesh.shape["tensor"] == 2
    return jax.shard_map(
        shards_planes if planes else shards_any,
        mesh=mesh,
        in_specs=placed,
        out_specs=(P("dp", None, "tensor"), P("dp", None, "tensor")),
        check_vma=False,
    )
```
